256 devices in a mesh: section: 4 (over z_lo), expert: 16 (over x, y), dp: 4 (over z_hi, core).
Axes of the slice: x: 4, y: 4, z: 8 (z_hi: 2, z_lo: 4; z = z_hi * 4 + z_lo), core: 2. Of those that a mesh axis runs over, the one named last changes fastest.
Arguments:
- inputs: bfloat16 [4, 512, 2048], P(None, 'expert'), may hold values from -6 to 6
- norm_gain: bfloat16 [4, 2048], P('section'), may hold values from 0.099609375 to 1.8984375
- gate_weight: bfloat16 [4, 2048, 49152], P('section', None, ('expert', 'dp')), may hold values from -0.125 to 0.125
- up_weight: bfloat16 [4, 2048, 49152], P('section', None, ('expert', 'dp')), may hold values from -0.125 to 0.125
- down_weight: bfloat16 [4, 49152, 2048], P('section', ('expert', 'dp')), may hold values from -0.0546875 to 0.0546875
- expert_ids: int32 [4, 4, 512, 1], P('section', None, 'expert'), may hold values from 0 to 3; in each aligned block of 32 rows (0 to 31, 32 to 63, ..., all dimensions but the last counted through in order) at most 12 rows name the same one
Outputs:
- layer_outputs: bfloat16 [4, 4, 512, 2048], P('section', None, 'expert')
The draws below stay inside these ranges and needn't reach their ends.
Inputs may be any that keep to these rules, and one draw needn't show every extreme that they name: `expert_ids`: among the 32 tokens of one device for one layer and block, no expert is named more than 12 times.
All inputs are finite; a program needn't handle non-finite values.
Results may differ from the reference program's by a relative error of at most 0.03.
Values may be sent and summed in bfloat16 or wider, within the bound.
A program may use at most 64 MiB of HBM per device.

```python
import math
import jax
import jax.numpy as jnp
import numpy as np
from jax import lax

D = 2048
FF_DEV = 768
SPANS = 4
TOK_CH = 32
LAYERS = 4
EXPERTS = 4
SPLIT = 4
FF = 12288
CAP = 12
TOKENS = 512
N_EXPERT = 16
N_DP = 4


def block_levels(stream_key, extent, shards, smallest, high):
    factor_of = 1.0
    for position, blocks in shards:
        steps = jax.random.uniform(jax.random.fold_in(jax.random.fold_in(stream_key, 6), position), (blocks,), jnp.float32, smallest / len(shards), high / len(shards))
        factor_of = factor_of * jnp.repeat(jnp.exp(steps), extent[position] // blocks).reshape((-1,) + (1,) * (len(extent) - 1 - position))
    return factor_of


def routed_block(stream_key, own, number, rows, number_of, top, reach, lean):
    ranking = jax.random.permutation(stream_key, number_of)
    crowded, ordinary = portions_of(number_of, rows * top, reach, lean, True), portions_of(number_of, rows * top, reach, lean, False)
    places = jnp.arange(number_of)

    def named(tallies, offset_by):
        used = int((tallies > 0).sum())
        fixed = max(1, used // 4)
        moved = fixed + (places - fixed + offset_by * (used - fixed)) % max(1, number_of - fixed)
        return jnp.zeros((number_of,), jnp.int32).at[ranking[jnp.where(places < fixed, places, moved)]].set(jnp.asarray(tallies, jnp.int32))

    tallies = jnp.where(number % 4 == 0, named(crowded, number // 4), named(ordinary, number - number // 4 - 1))
    mixed = jax.random.permutation(jax.random.fold_in(own, 3), number_of)
    donor, receiver = mixed[0:number_of // 2 * 2:2], mixed[1:number_of // 2 * 2:2]
    room = jnp.minimum(tallies[donor] - 1, reach - tallies[receiver]) // 2
    room = jnp.where((donor == ranking[0]) | (receiver == ranking[0]) | (tallies[receiver] == 0), 0, jnp.maximum(room, 0))
    moved = jax.random.randint(jax.random.fold_in(own, 4), (number_of // 2,), 0, 1 << 20) % (room + 1)
    tallies = tallies.at[donor].add(-moved).at[receiver].add(moved)
    items = jnp.searchsorted(jnp.cumsum(tallies), jnp.arange(rows * top), side="right").astype(jnp.int32)
    listing = items.reshape(top, rows).T
    listing = listing[jax.random.permutation(jax.random.fold_in(own, 1), rows)]
    offset_by = jax.random.randint(jax.random.fold_in(own, 2), (rows, 1), 0, top)
    return jnp.take_along_axis(listing, (jnp.arange(top)[None, :] + offset_by) % top, axis=1)


def portions_of(number_of, total, reach, slope, full):
    weights = [(1 << 20) // math.isqrt(rank ** slope) + 1 for rank in range(1, number_of + 1)]
    largest = reach if full else min(reach, max(-(-total // number_of), total * weights[0] // sum(weights)))
    least = 1 if total - largest >= number_of - 1 else 0
    given, spare = [largest] + [least] * (number_of - 1), total - largest - least * (number_of - 1)
    while spare > 0:
        candidates = [i for i in range(1, number_of) if given[i] < largest] or [i for i in range(1, number_of) if given[i] < reach]
        pool, budget = sum([weights[i] for i in candidates]), spare
        for i in candidates:
            addition = min(reach - given[i], max(1, budget * weights[i] // pool), spare)
            given[i] = given[i] + addition
            spare = spare - addition
    return np.array(given)


def bell_draw(stream_key, dims, scale, bound, cuts=(), kind=jnp.bfloat16):
    level = block_levels(stream_key, dims, cuts, -0.22, 0.18) if cuts else 1.0
    array = jax.random.normal(stream_key, dims, jnp.float32) * scale * level
    return jnp.minimum(jnp.maximum(array, -bound), bound).astype(kind)


def setup_inputs(seed: int = 0) -> dict:
    key_list = jax.random.split(jax.random.key(seed), 7)
    inputs = bell_draw(key_list[0], (SPANS, TOKENS, D), 1.0, 6.0, ((1, 16),))
    norm_gain = jnp.clip(1.0 + 0.18 * jax.random.normal(key_list[1], (LAYERS, D), jnp.float32), 0.099609375, 1.8984375).astype(jnp.bfloat16)
    gate_weight = bell_draw(key_list[2], (LAYERS, D, EXPERTS * FF), D ** -0.5, 0.125, ((0, 4), (2, 64)))
    up_weight = bell_draw(key_list[3], (LAYERS, D, EXPERTS * FF), D ** -0.5, 0.125, ((0, 4), (2, 64)))
    down_weight = bell_draw(key_list[4], (LAYERS, EXPERTS * FF, D), FF ** -0.5, 0.0546875, ((0, 4), (1, 64)))
    expert_ids_keys = jax.random.split(jax.random.fold_in(key_list[5], 1), LAYERS * SPANS * TOKENS // TOK_CH)
    expert_ids_turns = jax.random.permutation(jax.random.fold_in(key_list[5], 3), LAYERS * SPANS * TOKENS // TOK_CH)
    expert_ids = jax.vmap(lambda own, number: routed_block(jax.random.fold_in(key_list[5], 2), own, number, TOK_CH, EXPERTS, 1, CAP, 1))(expert_ids_keys, expert_ids_turns).reshape((LAYERS, SPANS, TOKENS, 1))
    return {"inputs": inputs, "norm_gain": norm_gain, "gate_weight": gate_weight, "up_weight": up_weight, "down_weight": down_weight, "expert_ids": expert_ids}


def apply_layer(h, gain, w_gate, w_up, w_down, ids, tri):
    hf = h.astype(jnp.float32)
    scale = lax.rsqrt(lax.optimization_barrier(jnp.mean(hf * hf, axis=-1, keepdims=True)) + 1e-05)
    normed = (hf * scale * gain.astype(jnp.float32)).astype(jnp.bfloat16)
    blocks = normed.reshape(N_EXPERT, TOK_CH, D).astype(jnp.float32)
    groups = ids.reshape(N_EXPERT, TOK_CH)
    onehot = (groups[..., None] == jnp.arange(EXPERTS, dtype=jnp.int32)).astype(jnp.float32)
    earlier = jnp.einsum('st,bte->bse', tri, onehot)
    rank = lax.optimization_barrier(jnp.sum(earlier * onehot, axis=-1))
    slots = (rank[..., None] == jnp.arange(CAP).astype(jnp.float32)).astype(jnp.float32)
    place = jnp.einsum('bte,btc->ebct', onehot, slots)
    shares = SPLIT * N_DP
    total = jnp.zeros((N_EXPERT, TOK_CH, D), jnp.float32)
    for expert in range(EXPERTS):
        rows = jnp.einsum('bct,btd->bcd', place[expert], blocks).astype(jnp.bfloat16).reshape(N_EXPERT * CAP, D)
        first = expert * FF
        gate = jnp.dot(rows, w_gate[:, first:first + FF], preferred_element_type=jnp.float32)
        upper = jnp.dot(rows, w_up[:, first:first + FF], preferred_element_type=jnp.float32)
        active = (jax.nn.silu(gate) * upper).astype(jnp.bfloat16).reshape(N_EXPERT * CAP, shares, FF_DEV)
        down = w_down[first:first + FF].reshape(shares, FF_DEV, D)
        parts = jnp.einsum('nsf,sfd->nsd', active.astype(jnp.float32), down.astype(jnp.float32)).astype(jnp.bfloat16)
        summed = lax.optimization_barrier(jnp.sum(parts.astype(jnp.float32), axis=1)).reshape(N_EXPERT, CAP, D)
        total = total + jnp.einsum('bct,bcd->btd', place[expert], summed)
    return (hf + total.reshape(TOKENS, D)).astype(jnp.bfloat16)

def reference(inputs, norm_gain, gate_weight, up_weight, down_weight, expert_ids):
    tri = (jnp.arange(TOK_CH)[:, None] > jnp.arange(TOK_CH)[None, :]).astype(jnp.float32)
    stream = inputs
    layers_all = []
    for layer in range(LAYERS):
        blocks_new = []
        for block in range(SPANS):
            blocks_new.append(apply_layer(stream[block], norm_gain[layer], gate_weight[layer], up_weight[layer], down_weight[layer], expert_ids[layer, block, :, 0], tri))
        stream = jnp.stack(blocks_new)
        layers_all.append(stream)
    return jnp.stack(layers_all)
```

```python
import functools

import jax
import jax.numpy as jnp
import numpy as np
from jax import lax
from jax.experimental import pallas as pl
from jax.experimental.pallas import tpu as pltpu
from jax.sharding import PartitionSpec as P

MESH = pl.DeviceIdType.MESH
EXPERTS = 4
CHUNKS = 4
F32 = jnp.float32
BF16 = jnp.bfloat16


def dist(shift, size):
    return min(shift, size - shift)


def wait_bytes(ref, sem):
    pltpu.make_async_copy(ref, ref, sem).wait()


def kernel(
    n_section,
    split,
    cap,
    x_ref,
    ids_ref,
    gain_ref,
    tgt_col_ref,
    tgt_row_ref,
    perm_ref,
    perm_t_ref,
    wg_hbm,
    wu_hbm,
    wd_hbm,
    out_ref,
    wg,
    wu,
    wd,
    gain,
    place,
    place_t,
    hbuf,
    dsend,
    drecv,
    dother,
    rows,
    act,
    csend,
    crecv,
    own,
    packed,
    rsend,
    rrecv,
    hsend,
    hrecv,
    zrecv,
    ostage,
    obuf,
    wsem,
    dsend_sem,
    drecv_sem,
    fsend_sem,
    frecv_sem,
    csend_sem,
    crecv_sem,
    rsend_sem,
    rrecv_sem,
    hsend_sem,
    hrecv_sem,
    zsend_sem,
    zrecv_sem,
    osend_sem,
    orecv_sem,
):
    spans, tok, width = x_ref.shape
    half = width // 2
    chunk = half // CHUNKS
    hidden = wg.shape[1]
    group = split * cap
    last = n_section - 1
    s = lax.axis_index("section")
    me = lax.axis_index("expert")
    d = lax.axis_index("dp")
    core, zh = d % 2, d // 2
    ex, ey = me // split, me % split
    other = {"dp": zh * 2 + 1 - core}
    across = {"dp": (1 - zh) * 2 + core}

    mine = pl.ds(pl.multiple_of(core * half, half), half)
    theirs = pl.ds(pl.multiple_of((1 - core) * half, half), half)
    low, high = pl.ds(0, half), pl.ds(half, half)
    loads = []
    for side, (source, target) in enumerate(((mine, low), (theirs, high))):
        loads.append((wg_hbm.at[0, source], wg.at[target]))
        loads.append((wu_hbm.at[0, source], wu.at[target]))
        loads.append((wd_hbm.at[0, :, source], wd.at[side]))
    loads = [
        pltpu.make_async_copy(source, target, wsem.at[i])
        for i, (source, target) in enumerate(loads)
    ]
    for load in loads:
        load.start()

    shifts = sorted(
        ((jx, jy) for jx in range(EXPERTS) for jy in range(split) if jx or jy),
        key=lambda j: -dist(j[0], EXPERTS) - dist(j[1], split),
    )

    def peer(jx, jy):
        return {"expert": ((ex + jx) % EXPERTS) * split + (ey + jy) % split}

    barrier = pltpu.get_barrier_semaphore()

    def greet(device):
        pl.semaphore_signal(barrier, inc=1, device_id=device, device_id_type=MESH)

    def section_peers(section):
        return [
            {"section": section, "dp": zh * 2 + core},
            {"section": section, "dp": zh * 2 + 1 - core},
            {"section": section, "dp": (1 - zh) * 2 + core},
        ]

    for jx, jy in shifts:
        greet(peer(jx, jy))
    greet(other)
    greet(across)

    @pl.when(s < last)
    def _():
        for device in section_peers(s + 1):
            greet(device)

    @pl.when(s > 0)
    def _():
        for device in section_peers(s - 1):
            greet(device)

    gain[0] = gain_ref[:, mine].astype(F32)
    gain[1] = gain_ref[:, theirs].astype(F32)

    def placement(c, carry):
        n = CHUNKS * tok
        row = lax.broadcasted_iota(jnp.int32, (n, n), 0)
        col = lax.broadcasted_iota(jnp.int32, (n, n), 1)
        ids_col = ids_ref[c]
        ids_row = jnp.sum(jnp.where(row == col, ids_col, 0), axis=0, keepdims=True)
        same = (ids_col == ids_row) & (row // tok == col // tok)
        rank_row = jnp.sum((same & (row < col)).astype(jnp.int32), axis=0, keepdims=True)
        rank_col = jnp.sum((same & (col < row)).astype(jnp.int32), axis=1, keepdims=True)
        stride = EXPERTS * cap
        key_row = ids_row * cap + rank_row + stride * (col[0:1] // tok)
        key_col = ids_col * cap + rank_col + stride * (row[:, 0:1] // tok)
        place[c] = (tgt_col_ref[...] == key_row).astype(F32).astype(BF16)
        place_t[c] = (tgt_row_ref[...] == key_col).astype(F32).astype(BF16)
        return carry

    lax.fori_loop(0, spans, placement, 0)

    expected = len(shifts) + 2 + 3 * (s < last).astype(jnp.int32) + 3 * (s > 0).astype(jnp.int32)
    pl.semaphore_wait(barrier, expected)

    def remote(source, target, send_sem, recv_sem, device):
        pltpu.make_async_remote_copy(
            src_ref=source,
            dst_ref=target,
            send_sem=send_sem,
            recv_sem=recv_sem,
            device_id=device,
            device_id_type=MESH,
        ).start()

    def dispatch(c):
        @pl.when(s == 0)
        def _():
            for q in range(CHUNKS):
                cols = pl.ds(pl.multiple_of(core * half + q * chunk, chunk), chunk)
                hbuf[c, q * tok : (q + 1) * tok] = x_ref[c, :, cols]

        @pl.when(s > 0)
        def _():
            wait_bytes(hrecv.at[c], hrecv_sem.at[c])
            hbuf[c] = (hrecv[c, 0].astype(F32) + hrecv[c, 1].astype(F32)).astype(BF16)

        sent = jnp.dot(place[c], hbuf[c], preferred_element_type=F32).astype(BF16)
        dsend[c] = sent.reshape(EXPERTS, CHUNKS * cap, chunk)
        for jx, jy in shifts:
            ix, iy = (-jx) % EXPERTS, (-jy) % split
            remote(
                dsend.at[c, (ex + jx) % EXPERTS],
                drecv.at[c, ix, iy],
                dsend_sem.at[c],
                drecv_sem.at[c, ix],
                peer(jx, jy),
            )
        pltpu.make_async_copy(dsend.at[c, ex], drecv.at[c, 0, 0], drecv_sem.at[c, 0]).start()

        @pl.when(s > 0)
        def _():
            for q in range(CHUNKS):
                ostage[c, :, q * chunk : (q + 1) * chunk] = hbuf[c, q * tok : (q + 1) * tok]
            for k in range(2):
                remote(
                    ostage.at[c],
                    obuf.at[c, core],
                    osend_sem.at[c],
                    orecv_sem.at[c],
                    {"section": s - 1, "dp": zh * 2 + k},
                )

    def unpack(source, i, side):
        z = jnp.dot(
            perm_ref[...], source.reshape(split * CHUNKS * cap, chunk), preferred_element_type=F32
        )
        total = jnp.zeros((group, 1), F32)
        for q in range(CHUNKS):
            part = z[q * group : (q + 1) * group]
            cols = slice(q * chunk, (q + 1) * chunk)
            place_at = slice(side * half + q * chunk, side * half + (q + 1) * chunk)
            rows[i * group : (i + 1) * group, place_at] = (part * gain[side, :, cols]).astype(BF16)
            total = total + jnp.sum(part * part, axis=1, keepdims=True)
        return total

    nearest = sorted(range(EXPERTS), key=lambda i: dist(i, EXPERTS))

    def experts(c):
        squares = [None] * EXPERTS
        for i in nearest:
            wait_bytes(drecv.at[c, i], drecv_sem.at[c, i])
            remote(drecv.at[c, i], dother.at[c, i], fsend_sem.at[c], frecv_sem.at[c, i], other)
            squares[i] = unpack(drecv[c, i], i, 0)
        for i in nearest:
            wait_bytes(dother.at[c, i], frecv_sem.at[c, i])
            squares[i] = squares[i] + unpack(dother[c, i], i, 1)
        scale = lax.rsqrt(jnp.concatenate(squares, axis=0) / width + 1e-5)
        for j in range(hidden // 256):
            cols = slice(j * 256, (j + 1) * 256)
            gate = jnp.dot(rows[...], wg[:, cols], preferred_element_type=F32) * scale
            upper = jnp.dot(rows[...], wu[:, cols], preferred_element_type=F32) * scale
            act[:, cols] = (gate / (1.0 + jnp.exp(-gate)) * upper).astype(BF16)
        for q in range(CHUNKS):
            cols = slice(q * chunk, (q + 1) * chunk)
            csend[c, q] = jnp.dot(act[...], wd[1, :, cols], preferred_element_type=F32).astype(BF16)
            remote(csend.at[c, q], crecv.at[c, q], csend_sem.at[c], crecv_sem.at[c, q], other)
        for q in range(CHUNKS):
            cols = slice(q * chunk, (q + 1) * chunk)
            own[q] = jnp.dot(act[...], wd[0, :, cols], preferred_element_type=F32)
        for q in range(CHUNKS):
            wait_bytes(crecv.at[c, q], crecv_sem.at[c, q])
            both = (own[q] + crecv[c, q].astype(F32)).astype(BF16)
            for i in range(EXPERTS):
                packed[i, q] = both[i * group : (i + 1) * group]
        for i in reversed(nearest):
            out = jnp.dot(
                perm_t_ref[...],
                packed[i].reshape(CHUNKS * group, chunk),
                preferred_element_type=F32,
            ).astype(BF16)
            rsend[c, i] = out.reshape(split, CHUNKS * cap, chunk)
            for jx, jy in shifts:
                if jx == i:
                    iy = (-jy) % split
                    remote(
                        rsend.at[c, jx, jy],
                        rrecv.at[c, ex, iy],
                        rsend_sem.at[c],
                        rrecv_sem.at[c],
                        peer(jx, jy),
                    )
        pltpu.make_async_copy(rsend.at[c, 0, 0], rrecv.at[c, ex, 0], rrecv_sem.at[c]).start()

    def combine(c):
        wait_bytes(rrecv.at[c], rrecv_sem.at[c])
        back = rrecv[c].reshape(EXPERTS * split * CHUNKS * cap, chunk)
        update = jnp.dot(place_t[c], back, preferred_element_type=F32)
        base = hbuf[c].astype(F32) * (zh == 0).astype(F32)
        hsend[c] = (base + update).astype(BF16)

        @pl.when(s < last)
        def _():
            for k in range(2):
                remote(
                    hsend.at[c],
                    hrecv.at[c, zh],
                    hsend_sem.at[c],
                    hrecv_sem.at[c],
                    {"section": s + 1, "dp": k * 2 + core},
                )

        @pl.when(s == last)
        def _():
            remote(hsend.at[c], zrecv.at[c], zsend_sem.at[c], zrecv_sem.at[c], across)

    def finish(c):
        wait_bytes(zrecv.at[c], zrecv_sem.at[c])
        whole = (hsend[c].astype(F32) + zrecv[c].astype(F32)).astype(BF16)
        for q in range(CHUNKS):
            obuf[c, core, :, q * chunk : (q + 1) * chunk] = whole[q * tok : (q + 1) * tok]
        remote(obuf.at[c, core], obuf.at[c, core], osend_sem.at[c], orecv_sem.at[c], other)

    def tick(t, carry):
        @pl.when(t < spans)
        def _():
            dispatch(t)

        @pl.when(t == 1)
        def _():
            for load in loads:
                load.wait()

        @pl.when((t >= 1) & (t < spans + 1))
        def _():
            experts(t - 1)

        @pl.when((t >= 2) & (t < spans + 2))
        def _():
            combine(t - 2)

        @pl.when((t >= 3) & (s == last))
        def _():
            finish(t - 3)

        return carry

    lax.fori_loop(0, spans + 3, tick, 0)

    def drain(c, carry):
        everyone = pl.ds(0, split - 1)
        wait_bytes(drecv.at[c, pl.ds(0, EXPERTS - 1)], dsend_sem.at[c])
        wait_bytes(drecv.at[c, EXPERTS - 1, everyone], dsend_sem.at[c])
        wait_bytes(drecv.at[c, pl.ds(0, EXPERTS - 1)], rsend_sem.at[c])
        wait_bytes(drecv.at[c, EXPERTS - 1, everyone], rsend_sem.at[c])
        wait_bytes(drecv.at[c], fsend_sem.at[c])
        wait_bytes(csend.at[c], csend_sem.at[c])

        @pl.when(s < last)
        def _():
            wait_bytes(hrecv.at[c], hsend_sem.at[c])
            wait_bytes(obuf.at[c], orecv_sem.at[c])

        @pl.when(s == last)
        def _():
            wait_bytes(hsend.at[c], zsend_sem.at[c])
            wait_bytes(ostage.at[c], osend_sem.at[c])
            wait_bytes(ostage.at[c], orecv_sem.at[c])

        @pl.when(s > 0)
        def _():
            wait_bytes(obuf.at[c], osend_sem.at[c])

        out_ref[0, c, :, 0:half] = obuf[c, 0]
        out_ref[0, c, :, half:width] = obuf[c, 1]
        return carry

    lax.fori_loop(0, spans, drain, 0)


def shards(inputs, norm_gain, gate_weight, up_weight, down_weight, expert_ids):
    n_section = lax.axis_size("section")
    n_expert = lax.axis_size("expert")
    split = n_expert // EXPERTS
    spans, tok, width = inputs.shape
    hidden = gate_weight.shape[-1]
    cap = tok // EXPERTS * 3 // 2
    half = width // 2
    chunk = half // CHUNKS
    group = split * cap
    total = EXPERTS * group
    block = CHUNKS * cap

    stride = EXPERTS * cap
    e, q, r = np.meshgrid(np.arange(EXPERTS), np.arange(CHUNKS), np.arange(cap), indexing="ij")
    key = (e * cap + r + stride * q).reshape(EXPERTS, block)
    tgt_col = key.reshape(-1, 1).astype(np.int32)
    tgt_row = np.repeat(key[:, None], split, axis=1).reshape(1, -1).astype(np.int32)
    order = np.arange(split * block).reshape(split, CHUNKS, cap).transpose(1, 0, 2).reshape(-1)
    perm = np.eye(split * block, dtype=np.float32)[order]
    ids = jnp.tile(expert_ids[0], (1, CHUNKS, 1))

    vmem = pl.BlockSpec(memory_space=pltpu.VMEM)
    hbm = pl.BlockSpec(memory_space=pl.ANY)
    dma = pltpu.SemaphoreType.DMA
    blocks = (spans, EXPERTS, split, block, chunk)
    return pl.pallas_call(
        functools.partial(kernel, n_section, split, cap),
        out_shape=jax.ShapeDtypeStruct((1, spans, tok, width), BF16),
        in_specs=[vmem] * 7 + [hbm] * 3,
        out_specs=vmem,
        scratch_shapes=[
            pltpu.VMEM((width, hidden), BF16),
            pltpu.VMEM((width, hidden), BF16),
            pltpu.VMEM((2, hidden, half), BF16),
            pltpu.VMEM((2, 1, half), F32),
            pltpu.VMEM((spans, EXPERTS * block, CHUNKS * tok), BF16),
            pltpu.VMEM((spans, CHUNKS * tok, EXPERTS * split * block), BF16),
            pltpu.VMEM((spans, CHUNKS * tok, chunk), BF16),
            pltpu.VMEM((spans, EXPERTS, block, chunk), BF16),
            pltpu.VMEM(blocks, BF16),
            pltpu.VMEM(blocks, BF16),
            pltpu.VMEM((total, width), BF16),
            pltpu.VMEM((total, hidden), BF16),
            pltpu.VMEM((spans, CHUNKS, total, chunk), BF16),
            pltpu.VMEM((spans, CHUNKS, total, chunk), BF16),
            pltpu.VMEM((CHUNKS, total, chunk), F32),
            pltpu.VMEM((EXPERTS, CHUNKS, group, chunk), BF16),
            pltpu.VMEM(blocks, BF16),
            pltpu.VMEM(blocks, BF16),
            pltpu.VMEM((spans, CHUNKS * tok, chunk), BF16),
            pltpu.VMEM((spans, 2, CHUNKS * tok, chunk), BF16),
            pltpu.VMEM((spans, CHUNKS * tok, chunk), BF16),
            pltpu.VMEM((spans, tok, half), BF16),
            pltpu.VMEM((spans, 2, tok, half), BF16),
            dma((6,)),
            dma((spans,)),
            dma((spans, EXPERTS)),
            dma((spans,)),
            dma((spans, EXPERTS)),
            dma((spans,)),
            dma((spans, CHUNKS)),
            dma((spans,)),
            dma((spans,)),
            dma((spans,)),
            dma((spans,)),
            dma((spans,)),
            dma((spans,)),
            dma((spans,)),
            dma((spans,)),
        ],
        compiler_params=pltpu.CompilerParams(
            collective_id=0, has_side_effects=True, vmem_limit_bytes=56 * 2**20
        ),
        name="layers",
    )(
        inputs,
        ids,
        norm_gain,
        jnp.asarray(tgt_col),
        jnp.asarray(tgt_row),
        jnp.asarray(perm, BF16),
        jnp.asarray(perm.T, BF16),
        gate_weight,
        up_weight,
        down_weight,
    )


def solution(mesh):
    placed = (
        P(None, "expert", None),
        P("section", None),
        P("section", None, ("expert", "dp")),
        P("section", None, ("expert", "dp")),
        P("section", ("expert", "dp"), None),
        P("section", None, "expert", None),
    )
    return jax.shard_map(
        shards,
        mesh=mesh,
        in_specs=placed,
        out_specs=P("section", None, "expert", None),
        check_vma=False,
    )
```

```python
import functools

import jax
import jax.numpy as jnp
import numpy as np
from jax import lax
from jax.experimental import pallas as pl
from jax.experimental.pallas import tpu as pltpu
from jax.sharding import PartitionSpec as P

MESH = pl.DeviceIdType.MESH
EXPERTS = 4
CHUNKS = 4
GROUP = 4
SHIFTS = [
    *((2, 2), (1, 2), (2, 3), (1, 3)),
    *((2, 1), (3, 2), (2, 0), (0, 2)),
    *((1, 1), (3, 3), (1, 0), (0, 3)),
    *((3, 1), (0, 1), (3, 0)),
]
F32 = jnp.float32
BF16 = jnp.bfloat16


def wait_bytes(ref, sem):
    pltpu.make_async_copy(ref, ref, sem).wait()


def kernel(
    n_section,
    split,
    cap,
    x_ref,
    ids_ref,
    gain_ref,
    tgt_col_ref,
    tgt_row_ref,
    perm_ref,
    perm_t_ref,
    wg_hbm,
    wu_hbm,
    wd_hbm,
    out_ref,
    wg,
    wu,
    wd,
    gain,
    place,
    place_t,
    hbuf,
    dsend,
    drecv,
    dother,
    rows,
    squares,
    act,
    csend,
    crecv,
    own,
    packed,
    rsend,
    rrecv,
    hsend,
    hrecv,
    zrecv,
    ostage,
    obuf,
    wsem,
    dsend_sem,
    drecv_sem,
    fsend_sem,
    frecv_sem,
    csend_sem,
    crecv_sem,
    rsend_sem,
    rrecv_sem,
    hsend_sem,
    hrecv_sem,
    zsend_sem,
    zrecv_sem,
    osend_sem,
    orecv_sem,
):
    spans, tok, width = x_ref.shape
    half = width // 2
    chunk = half // CHUNKS
    hidden = wg.shape[1]
    group = GROUP * cap
    last = n_section - 1
    s = lax.axis_index("section")
    me = lax.axis_index("expert")
    d = lax.axis_index("dp")
    core, zh = d % 2, d // 2
    ex, ey = me // split, me % split
    other = {"dp": zh * 2 + 1 - core}
    across = {"dp": (1 - zh) * 2 + core}
    opposite = {"dp": (1 - zh) * 2 + 1 - core}

    mine = pl.ds(pl.multiple_of(core * half, half), half)
    theirs = pl.ds(pl.multiple_of((1 - core) * half, half), half)
    low, high = pl.ds(0, half), pl.ds(half, half)
    loads = []
    for side, (source, target) in enumerate(((mine, low), (theirs, high))):
        loads.append((wg_hbm.at[0, source], wg.at[target]))
        loads.append((wu_hbm.at[0, source], wu.at[target]))
        loads.append((wd_hbm.at[0, :, source], wd.at[side]))
    loads = [
        pltpu.make_async_copy(source, target, wsem.at[i])
        for i, (source, target) in enumerate(loads)
    ]
    for load in loads:
        load.start()

    shifts = SHIFTS
    turned = [(-jy % split, -jx % EXPERTS) for jx, jy in shifts]

    def by_core(a, b):
        return a + core * (b - a)

    def sending(k):
        (jx, jy), (kx, ky) = shifts[k], turned[k]
        return by_core(k, shifts.index(turned[k])), by_core(jx, kx), by_core(jy, ky)

    n_shift = len(shifts)
    groups = (n_shift + 1) // GROUP

    def peer(jx, jy):
        return {"expert": ((ex + jx + EXPERTS) % EXPERTS) * split + (ey + jy + split) % split}

    barrier = pltpu.get_barrier_semaphore()

    def greet(device):
        pl.semaphore_signal(barrier, inc=1, device_id=device, device_id_type=MESH)

    def section_peers(section):
        return [
            {"section": section, "dp": zh * 2 + core},
            {"section": section, "dp": zh * 2 + 1 - core},
            {"section": section, "dp": (1 - zh) * 2 + core},
        ]

    for jx, jy in shifts:
        greet(peer(jx, jy))
    greet(other)
    greet(across)
    greet(opposite)

    @pl.when(s < last)
    def _():
        for device in section_peers(s + 1):
            greet(device)

    @pl.when(s > 0)
    def _():
        for device in section_peers(s - 1):
            greet(device)

    gain[0] = gain_ref[:, mine].astype(F32)
    gain[1] = gain_ref[:, theirs].astype(F32)

    def placement(c, carry):
        n = CHUNKS * tok
        row = lax.broadcasted_iota(jnp.int32, (n, n), 0)
        col = lax.broadcasted_iota(jnp.int32, (n, n), 1)
        token = lax.broadcasted_iota(jnp.int32, (n, tok), 0) % tok
        listed = lax.broadcasted_iota(jnp.int32, (n, tok), 1)
        ids_col = jnp.sum(jnp.where(token == listed, ids_ref[0, c], 0), axis=1, keepdims=True)
        ids_row = jnp.sum(jnp.where(row == col, ids_col, 0), axis=0, keepdims=True)
        same = (ids_col == ids_row) & (row // tok == col // tok)
        rank_row = jnp.sum((same & (row < col)).astype(jnp.int32), axis=0, keepdims=True)
        rank_col = jnp.sum((same & (col < row)).astype(jnp.int32), axis=1, keepdims=True)
        stride = EXPERTS * cap
        key_row = ids_row * cap + rank_row + stride * (col[0:1] // tok)
        key_col = ids_col * cap + rank_col + stride * (row[:, 0:1] // tok)
        place[c] = (tgt_col_ref[...] == key_row).astype(F32).astype(BF16)
        place_t[c] = (tgt_row_ref[...] == key_col).astype(F32).astype(BF16)
        return carry

    lax.fori_loop(0, spans, placement, 0)

    expected = len(shifts) + 3 + 3 * (s < last).astype(jnp.int32) + 3 * (s > 0).astype(jnp.int32)
    pl.semaphore_wait(barrier, expected)

    def remote(source, target, send_sem, recv_sem, device):
        pltpu.make_async_remote_copy(
            src_ref=source,
            dst_ref=target,
            send_sem=send_sem,
            recv_sem=recv_sem,
            device_id=device,
            device_id_type=MESH,
        ).start()

    def dispatch(c):
        @pl.when(s == 0)
        def _():
            for q in range(CHUNKS):
                cols = pl.ds(pl.multiple_of(core * half + q * chunk, chunk), chunk)
                hbuf[c, q * tok : (q + 1) * tok] = x_ref[c, :, cols]

        @pl.when(s > 0)
        def _():
            wait_bytes(hrecv.at[c], hrecv_sem.at[c])
            hbuf[c] = (hrecv[c, 0].astype(F32) + hrecv[c, 1].astype(F32)).astype(BF16)

        sent = jnp.dot(place[c], hbuf[c], preferred_element_type=F32).astype(BF16)
        dsend[c] = sent.reshape(EXPERTS, CHUNKS * cap, chunk)
        for k in range(n_shift):
            slot, jx, jy = sending(k)
            remote(
                dsend.at[c, (ex + jx) % EXPERTS],
                drecv.at[c, slot],
                dsend_sem.at[c],
                drecv_sem.at[c, k // GROUP],
                peer(jx, jy),
            )
        pltpu.make_async_copy(
            dsend.at[c, ex], drecv.at[c, n_shift], drecv_sem.at[c, groups - 1]
        ).start()

        @pl.when(s > 0)
        def _():
            for q in range(CHUNKS):
                ostage[c, :, q * chunk : (q + 1) * chunk] = hbuf[c, q * tok : (q + 1) * tok]
            for k in range(2):
                remote(
                    ostage.at[c],
                    obuf.at[c, core],
                    osend_sem.at[c],
                    orecv_sem.at[c],
                    {"section": s - 1, "dp": zh * 2 + k},
                )

    def unpack(source, i, side):
        z = jnp.dot(
            perm_ref[...], source.reshape(GROUP * CHUNKS * cap, chunk), preferred_element_type=F32
        )
        total = jnp.zeros((group, 1), F32)
        for q in range(CHUNKS):
            part = z[q * group : (q + 1) * group]
            cols = slice(q * chunk, (q + 1) * chunk)
            place_at = slice(side * half + q * chunk, side * half + (q + 1) * chunk)
            rows[i * group : (i + 1) * group, place_at] = (part * gain[side, :, cols]).astype(BF16)
            total = total + jnp.sum(part * part, axis=1, keepdims=True)
        return total

    def gather(c):
        for i in range(groups):
            here = pl.ds(i * GROUP, GROUP)
            wait_bytes(drecv.at[c, here], drecv_sem.at[c, i])
            remote(drecv.at[c, here], dother.at[c, here], fsend_sem.at[c], frecv_sem.at[c, i], other)
            squares[i] = unpack(drecv[c, i * GROUP : (i + 1) * GROUP], i, 0)

    def gather_other(c):
        for i in range(groups):
            here = pl.ds(i * GROUP, GROUP)
            wait_bytes(dother.at[c, here], frecv_sem.at[c, i])
            squares[i] = squares[i] + unpack(dother[c, i * GROUP : (i + 1) * GROUP], i, 1)

    def experts(c):
        total = squares[...].reshape(groups * group, 1)
        scale = lax.rsqrt(total / width + 1e-5)
        for j in range(hidden // 256):
            cols = slice(j * 256, (j + 1) * 256)
            gate = jnp.dot(rows[...], wg[:, cols], preferred_element_type=F32) * scale
            upper = jnp.dot(rows[...], wu[:, cols], preferred_element_type=F32) * scale
            act[:, cols] = (gate / (1.0 + jnp.exp(-gate)) * upper).astype(BF16)
        for q in range(CHUNKS):
            cols = slice(q * chunk, (q + 1) * chunk)
            csend[c, q] = jnp.dot(act[...], wd[1, :, cols], preferred_element_type=F32).astype(BF16)
            remote(csend.at[c, q], crecv.at[c, q], csend_sem.at[c], crecv_sem.at[c, q], other)

    def down(c):
        for q in range(CHUNKS):
            cols = slice(q * chunk, (q + 1) * chunk)
            own[q] = jnp.dot(act[...], wd[0, :, cols], preferred_element_type=F32)

    def give_back(c):
        for q in range(CHUNKS):
            wait_bytes(crecv.at[c, q], crecv_sem.at[c, q])
            both = (own[q] + crecv[c, q].astype(F32)).astype(BF16)
            for i in range(groups):
                packed[i, q] = both[i * group : (i + 1) * group]
        for i in range(groups):
            out = jnp.dot(
                perm_t_ref[...],
                packed[i].reshape(CHUNKS * group, chunk),
                preferred_element_type=F32,
            ).astype(BF16)
            rsend[c, i * GROUP : (i + 1) * GROUP] = out.reshape(GROUP, CHUNKS * cap, chunk)
            for k in range(i * GROUP, min(n_shift, (i + 1) * GROUP)):
                slot, jx, jy = sending(k)
                remote(
                    rsend.at[c, slot],
                    rrecv.at[c, ex, ey],
                    rsend_sem.at[c],
                    rrecv_sem.at[c],
                    peer(-jx, -jy),
                )
        pltpu.make_async_copy(rsend.at[c, n_shift], rrecv.at[c, ex, ey], rrecv_sem.at[c]).start()

    def combine(c):
        wait_bytes(rrecv.at[c], rrecv_sem.at[c])
        back = rrecv[c].reshape(EXPERTS * split * CHUNKS * cap, chunk)
        update = jnp.dot(place_t[c], back, preferred_element_type=F32)
        base = hbuf[c].astype(F32) * (zh == 0).astype(F32)
        hsend[c] = (base + update).astype(BF16)

        @pl.when(s < last)
        def _():
            for k in range(2):
                remote(
                    hsend.at[c],
                    hrecv.at[c, zh],
                    hsend_sem.at[c],
                    hrecv_sem.at[c],
                    {"section": s + 1, "dp": (1 - zh if k == 0 else zh) * 2 + core},
                )

        @pl.when(s == last)
        def _():
            zrecv[c, d] = hsend[c]
            for device in (across, opposite, other):
                remote(
                    hsend.at[c], zrecv.at[c, d], zsend_sem.at[c], zrecv_sem.at[c], device
                )

    def finish(c):
        wait_bytes(zrecv.at[c, pl.ds(0, 3)], zrecv_sem.at[c])
        for k in range(2):
            whole = (zrecv[c, k].astype(F32) + zrecv[c, 2 + k].astype(F32)).astype(BF16)
            for q in range(CHUNKS):
                obuf[c, k, :, q * chunk : (q + 1) * chunk] = whole[q * tok : (q + 1) * tok]

    def load_wait(c):
        @pl.when(c == 0)
        def _():
            for load in loads:
                load.wait()

    def last_only(c):
        @pl.when(s == last)
        def _():
            finish(c)

    def step(t, lag, phase):
        @pl.when((t >= lag) & (t < spans + lag))
        def _():
            phase(t - lag)

    def tick(t, carry):
        step(t, 1, gather)
        step(t, 0, dispatch)
        step(t, 1, gather_other)
        step(t, 1, load_wait)
        step(t, 1, experts)
        step(t, 1, down)
        step(t, 2, combine)
        step(t, 1, give_back)
        step(t, 3, last_only)
        return carry

    lax.fori_loop(0, spans + 3, tick, 0)

    def drain(c, carry):
        wait_bytes(drecv.at[c, pl.ds(0, n_shift)], dsend_sem.at[c])
        wait_bytes(drecv.at[c, pl.ds(0, n_shift)], rsend_sem.at[c])
        wait_bytes(drecv.at[c], fsend_sem.at[c])
        wait_bytes(csend.at[c], csend_sem.at[c])

        @pl.when(s < last)
        def _():
            wait_bytes(hrecv.at[c], hsend_sem.at[c])
            wait_bytes(obuf.at[c], orecv_sem.at[c])

        @pl.when(s == last)
        def _():
            wait_bytes(zrecv.at[c, pl.ds(0, 3)], zsend_sem.at[c])

        @pl.when(s > 0)
        def _():
            wait_bytes(obuf.at[c], osend_sem.at[c])

        out_ref[0, c, :, 0:half] = obuf[c, 0]
        out_ref[0, c, :, half:width] = obuf[c, 1]
        return carry

    lax.fori_loop(0, spans, drain, 0)


def shards(inputs, norm_gain, gate_weight, up_weight, down_weight, expert_ids):
    n_section = lax.axis_size("section")
    n_expert = lax.axis_size("expert")
    split = n_expert // EXPERTS
    spans, tok, width = inputs.shape
    hidden = gate_weight.shape[-1]
    cap = tok // EXPERTS * 3 // 2
    half = width // 2
    chunk = half // CHUNKS
    group = GROUP * cap
    total = n_expert * cap
    block = CHUNKS * cap

    stride = EXPERTS * cap
    e, q, r = np.meshgrid(np.arange(EXPERTS), np.arange(CHUNKS), np.arange(cap), indexing="ij")
    key = (e * cap + r + stride * q).reshape(EXPERTS, block)
    tgt_col = key.reshape(-1, 1).astype(np.int32)
    tgt_row = np.repeat(key[:, None], split, axis=1).reshape(1, -1).astype(np.int32)
    order = np.arange(GROUP * block).reshape(GROUP, CHUNKS, cap).transpose(1, 0, 2).reshape(-1)
    perm = np.eye(GROUP * block, dtype=np.float32)[order]

    vmem = pl.BlockSpec(memory_space=pltpu.VMEM)
    hbm = pl.BlockSpec(memory_space=pl.ANY)
    dma = pltpu.SemaphoreType.DMA
    blocks = (spans, n_expert, block, chunk)
    return pl.pallas_call(
        functools.partial(kernel, n_section, split, cap),
        out_shape=jax.ShapeDtypeStruct((1, spans, tok, width), BF16),
        in_specs=[vmem] * 7 + [hbm] * 3,
        out_specs=vmem,
        scratch_shapes=[
            pltpu.VMEM((width, hidden), BF16),
            pltpu.VMEM((width, hidden), BF16),
            pltpu.VMEM((2, hidden, half), BF16),
            pltpu.VMEM((2, 1, half), F32),
            pltpu.VMEM((spans, EXPERTS * block, CHUNKS * tok), BF16),
            pltpu.VMEM((spans, CHUNKS * tok, EXPERTS * split * block), BF16),
            pltpu.VMEM((spans, CHUNKS * tok, chunk), BF16),
            pltpu.VMEM((spans, EXPERTS, block, chunk), BF16),
            pltpu.VMEM(blocks, BF16),
            pltpu.VMEM(blocks, BF16),
            pltpu.VMEM((total, width), BF16),
            pltpu.VMEM((total // group, group, 1), F32),
            pltpu.VMEM((total, hidden), BF16),
            pltpu.VMEM((spans, CHUNKS, total, chunk), BF16),
            pltpu.VMEM((spans, CHUNKS, total, chunk), BF16),
            pltpu.VMEM((CHUNKS, total, chunk), F32),
            pltpu.VMEM((total // group, CHUNKS, group, chunk), BF16),
            pltpu.VMEM(blocks, BF16),
            pltpu.VMEM((spans, EXPERTS, split, block, chunk), BF16),
            pltpu.VMEM((spans, CHUNKS * tok, chunk), BF16),
            pltpu.VMEM((spans, 2, CHUNKS * tok, chunk), BF16),
            pltpu.VMEM((spans, 4, CHUNKS * tok, chunk), BF16),
            pltpu.VMEM((spans, tok, half), BF16),
            pltpu.VMEM((spans, 2, tok, half), BF16),
            dma((6,)),
            dma((spans,)),
            dma((spans, total // group)),
            dma((spans,)),
            dma((spans, total // group)),
            dma((spans,)),
            dma((spans, CHUNKS)),
            dma((spans,)),
            dma((spans,)),
            dma((spans,)),
            dma((spans,)),
            dma((spans,)),
            dma((spans,)),
            dma((spans,)),
            dma((spans,)),
        ],
        compiler_params=pltpu.CompilerParams(
            collective_id=0, has_side_effects=True, vmem_limit_bytes=56 * 2**20
        ),
        name="layers",
    )(
        inputs,
        jnp.swapaxes(expert_ids, 2, 3),
        norm_gain,
        jnp.asarray(tgt_col),
        jnp.asarray(tgt_row),
        jnp.asarray(perm, BF16),
        jnp.asarray(perm.T, BF16),
        gate_weight,
        up_weight,
        down_weight,
    )


def solution(mesh):
    placed = (
        P(None, "expert", None),
        P("section", None),
        P("section", None, ("expert", "dp")),
        P("section", None, ("expert", "dp")),
        P("section", ("expert", "dp"), None),
        P("section", None, "expert", None),
    )
    return jax.shard_map(
        shards,
        mesh=mesh,
        in_specs=placed,
        out_specs=P("section", None, "expert", None),
        check_vma=False,
    )
```

```python
import functools

import jax
import jax.numpy as jnp
import numpy as np
from jax import lax
from jax.experimental import pallas as pl
from jax.experimental.pallas import tpu as pltpu
from jax.sharding import PartitionSpec as P

MESH = pl.DeviceIdType.MESH
EXPERTS = 4
CHUNKS = 4
GROUP = 4
SHIFTS = [
    *((2, 2), (1, 2), (2, 3), (1, 3)),
    *((2, 1), (3, 2), (2, 0), (0, 2)),
    *((1, 1), (3, 3), (1, 0), (0, 3)),
    *((3, 1), (0, 1), (3, 0)),
]
F32 = jnp.float32
BF16 = jnp.bfloat16


def wait_bytes(ref, sem):
    pltpu.make_async_copy(ref, ref, sem).wait()


def kernel(
    n_section,
    split,
    cap,
    x_ref,
    ids_ref,
    gain_ref,
    tgt_col_ref,
    tgt_row_ref,
    perm_ref,
    perm_t_ref,
    wg_hbm,
    wu_hbm,
    wd_hbm,
    out_ref,
    wg,
    wu,
    wd,
    gain,
    place,
    place_t,
    hbuf,
    dsend,
    drecv,
    dother,
    rows,
    squares,
    sums,
    act,
    csend,
    crecv,
    own,
    packed,
    rsend,
    rrecv,
    hsend,
    hrecv,
    zrecv,
    ostage,
    obuf,
    wsem,
    dsend_sem,
    drecv_sem,
    fsend_sem,
    frecv_sem,
    csend_sem,
    crecv_sem,
    rsend_sem,
    rrecv_sem,
    hsend_sem,
    hrecv_sem,
    zsend_sem,
    zrecv_sem,
    osend_sem,
    orecv_sem,
):
    spans, tok, width = x_ref.shape
    half = width // 2
    chunk = half // CHUNKS
    hidden = wg.shape[1]
    group = GROUP * cap
    last = n_section - 1
    s = lax.axis_index("section")
    me = lax.axis_index("expert")
    d = lax.axis_index("dp")
    core, zh = d % 2, d // 2
    ex, ey = me // split, me % split
    other = {"dp": zh * 2 + 1 - core}
    across = {"dp": (1 - zh) * 2 + core}
    opposite = {"dp": (1 - zh) * 2 + 1 - core}

    mine = pl.ds(pl.multiple_of(core * half, half), half)
    theirs = pl.ds(pl.multiple_of((1 - core) * half, half), half)
    low, high = pl.ds(0, half), pl.ds(half, half)
    loads = []
    for side, (source, target) in enumerate(((mine, low), (theirs, high))):
        loads.append((wg_hbm.at[0, source], wg.at[target]))
        loads.append((wu_hbm.at[0, source], wu.at[target]))
        loads.append((wd_hbm.at[0, :, source], wd.at[side]))
    loads = [
        pltpu.make_async_copy(source, target, wsem.at[i])
        for i, (source, target) in enumerate(loads)
    ]
    for load in loads:
        load.start()

    shifts = SHIFTS
    turned = [(-jy % split, -jx % EXPERTS) for jx, jy in shifts]

    def by_core(a, b):
        return a + core * (b - a)

    def sending(k):
        (jx, jy), (kx, ky) = shifts[k], turned[k]
        return by_core(k, shifts.index(turned[k])), by_core(jx, kx), by_core(jy, ky)

    n_shift = len(shifts)
    groups = (n_shift + 1) // GROUP

    def peer(jx, jy):
        return {"expert": ((ex + jx + EXPERTS) % EXPERTS) * split + (ey + jy + split) % split}

    barrier = pltpu.get_barrier_semaphore()

    def greet(device):
        pl.semaphore_signal(barrier, inc=1, device_id=device, device_id_type=MESH)

    def section_peers(section):
        return [
            {"section": section, "dp": zh * 2 + core},
            {"section": section, "dp": zh * 2 + 1 - core},
            {"section": section, "dp": (1 - zh) * 2 + core},
        ]

    for jx, jy in shifts:
        greet(peer(jx, jy))
    greet(other)
    greet(across)
    greet(opposite)

    @pl.when(s < last)
    def _():
        for device in section_peers(s + 1):
            greet(device)

    @pl.when(s > 0)
    def _():
        for device in section_peers(s - 1):
            greet(device)

    gain[0] = gain_ref[:, mine].astype(F32)
    gain[1] = gain_ref[:, theirs].astype(F32)

    def placement(c, carry):
        n = CHUNKS * tok
        row = lax.broadcasted_iota(jnp.int32, (n, n), 0)
        col = lax.broadcasted_iota(jnp.int32, (n, n), 1)
        token = lax.broadcasted_iota(jnp.int32, (n, tok), 0) % tok
        listed = lax.broadcasted_iota(jnp.int32, (n, tok), 1)
        ids_col = jnp.sum(jnp.where(token == listed, ids_ref[0, c], 0), axis=1, keepdims=True)
        ids_row = jnp.sum(jnp.where(row == col, ids_col, 0), axis=0, keepdims=True)
        same = (ids_col == ids_row) & (row // tok == col // tok)
        rank_row = jnp.sum((same & (row < col)).astype(jnp.int32), axis=0, keepdims=True)
        rank_col = jnp.sum((same & (col < row)).astype(jnp.int32), axis=1, keepdims=True)
        stride = EXPERTS * cap
        key_row = ids_row * cap + rank_row + stride * (col[0:1] // tok)
        key_col = ids_col * cap + rank_col + stride * (row[:, 0:1] // tok)
        place[c] = (tgt_col_ref[...] == key_row).astype(F32).astype(BF16)
        place_t[c] = (tgt_row_ref[...] == key_col).astype(F32).astype(BF16)
        return carry

    placement(0, 0)

    expected = len(shifts) + 3 + 3 * (s < last).astype(jnp.int32) + 3 * (s > 0).astype(jnp.int32)
    pl.semaphore_wait(barrier, expected)

    def remote(source, target, send_sem, recv_sem, device):
        pltpu.make_async_remote_copy(
            src_ref=source,
            dst_ref=target,
            send_sem=send_sem,
            recv_sem=recv_sem,
            device_id=device,
            device_id_type=MESH,
        ).start()

    def send_rows(c):
        sent = jnp.dot(place[c], hbuf[c], preferred_element_type=F32).astype(BF16)
        dsend[c] = sent.reshape(EXPERTS, CHUNKS * cap, chunk)
        for k in range(n_shift):
            slot, jx, jy = sending(k)
            remote(
                dsend.at[c, (ex + jx) % EXPERTS],
                drecv.at[c, slot],
                dsend_sem.at[c],
                drecv_sem.at[c, k // GROUP],
                peer(jx, jy),
            )
        pltpu.make_async_copy(
            dsend.at[c, ex], drecv.at[c, n_shift], drecv_sem.at[c, groups - 1]
        ).start()

    def dispatch_inputs(c):
        for q in range(CHUNKS):
            cols = pl.ds(pl.multiple_of(core * half + q * chunk, chunk), chunk)
            hbuf[c, q * tok : (q + 1) * tok] = x_ref[c, :, cols]
        send_rows(c)

    def dispatch(c):
        wait_bytes(hrecv.at[c], hrecv_sem.at[c])
        hbuf[c] = (hrecv[c, 0].astype(F32) + hrecv[c, 1].astype(F32)).astype(BF16)
        send_rows(c)
        for q in range(CHUNKS):
            ostage[c, :, q * chunk : (q + 1) * chunk] = hbuf[c, q * tok : (q + 1) * tok]
        for k in range(2):
            remote(
                ostage.at[c],
                obuf.at[c, core],
                osend_sem.at[c],
                orecv_sem.at[c],
                {"section": s - 1, "dp": zh * 2 + k},
            )

    def unpack(source, i, side):
        z = jnp.dot(
            perm_ref[...], source.reshape(GROUP * CHUNKS * cap, chunk), preferred_element_type=F32
        )
        total = jnp.zeros((group, 1), F32)
        for q in range(CHUNKS):
            part = z[q * group : (q + 1) * group]
            cols = slice(q * chunk, (q + 1) * chunk)
            place_at = slice(side * half + q * chunk, side * half + (q + 1) * chunk)
            rows[i * group : (i + 1) * group, place_at] = (part * gain[side, :, cols]).astype(BF16)
            total = total + jnp.sum(part * part, axis=1, keepdims=True)
        return total

    def gather(c):
        for i in range(groups):
            here = pl.ds(i * GROUP, GROUP)
            wait_bytes(drecv.at[c, here], drecv_sem.at[c, i])
            remote(drecv.at[c, here], dother.at[c, here], fsend_sem.at[c], frecv_sem.at[c, i], other)
            squares[i] = unpack(drecv[c, i * GROUP : (i + 1) * GROUP], i, 0)

    def gather_other(c):
        for i in range(groups):
            here = pl.ds(i * GROUP, GROUP)
            wait_bytes(dother.at[c, here], frecv_sem.at[c, i])
            squares[i] = squares[i] + unpack(dother[c, i * GROUP : (i + 1) * GROUP], i, 1)

    def experts_own(c):
        for j in range(hidden // 256):
            cols = slice(j * 256, (j + 1) * 256)
            sums[0, :, cols] = jnp.dot(
                rows[:, 0:half], wg[0:half, cols], preferred_element_type=F32
            )
            sums[1, :, cols] = jnp.dot(
                rows[:, 0:half], wu[0:half, cols], preferred_element_type=F32
            )

    def experts(c):
        total = squares[...].reshape(groups * group, 1)
        scale = lax.rsqrt(total / width + 1e-5)
        for j in range(hidden // 256):
            cols = slice(j * 256, (j + 1) * 256)
            gate = sums[0, :, cols] + jnp.dot(
                rows[:, half:width], wg[half:width, cols], preferred_element_type=F32
            )
            upper = sums[1, :, cols] + jnp.dot(
                rows[:, half:width], wu[half:width, cols], preferred_element_type=F32
            )
            gate = gate * scale
            act[:, cols] = (gate / (1.0 + jnp.exp(-gate)) * (upper * scale)).astype(BF16)
        for q in range(CHUNKS):
            cols = slice(q * chunk, (q + 1) * chunk)
            csend[c, q] = jnp.dot(act[...], wd[1, :, cols], preferred_element_type=F32).astype(BF16)
            remote(csend.at[c, q], crecv.at[c, q], csend_sem.at[c], crecv_sem.at[c, q], other)

    def down(c):
        for q in range(CHUNKS):
            cols = slice(q * chunk, (q + 1) * chunk)
            own[q] = jnp.dot(act[...], wd[0, :, cols], preferred_element_type=F32)

    def give_back(c):
        for q in range(CHUNKS):
            wait_bytes(crecv.at[c, q], crecv_sem.at[c, q])
            both = (own[q] + crecv[c, q].astype(F32)).astype(BF16)
            for i in range(groups):
                packed[i, q] = both[i * group : (i + 1) * group]
        for i in range(groups):
            out = jnp.dot(
                perm_t_ref[...],
                packed[i].reshape(CHUNKS * group, chunk),
                preferred_element_type=F32,
            ).astype(BF16)
            rsend[c, i * GROUP : (i + 1) * GROUP] = out.reshape(GROUP, CHUNKS * cap, chunk)
            for k in range(i * GROUP, min(n_shift, (i + 1) * GROUP)):
                slot, jx, jy = sending(k)
                remote(
                    rsend.at[c, slot],
                    rrecv.at[c, ex, ey],
                    rsend_sem.at[c],
                    rrecv_sem.at[c],
                    peer(-jx, -jy),
                )
        pltpu.make_async_copy(rsend.at[c, n_shift], rrecv.at[c, ex, ey], rrecv_sem.at[c]).start()

    def combine(c):
        wait_bytes(rrecv.at[c], rrecv_sem.at[c])
        back = rrecv[c].reshape(EXPERTS * split * CHUNKS * cap, chunk)
        update = jnp.dot(place_t[c], back, preferred_element_type=F32)
        base = hbuf[c].astype(F32) * (zh == 0).astype(F32)
        hsend[c] = (base + update).astype(BF16)

        @pl.when(s < last)
        def _():
            for k in range(2):
                remote(
                    hsend.at[c],
                    hrecv.at[c, zh],
                    hsend_sem.at[c],
                    hrecv_sem.at[c],
                    {"section": s + 1, "dp": (1 - zh if k == 0 else zh) * 2 + core},
                )

        @pl.when(s == last)
        def _():
            zrecv[c, d] = hsend[c]
            for device in (across, opposite, other):
                remote(
                    hsend.at[c], zrecv.at[c, d], zsend_sem.at[c], zrecv_sem.at[c], device
                )

    def finish(c):
        wait_bytes(zrecv.at[c, pl.ds(0, 3)], zrecv_sem.at[c])
        for k in range(2):
            whole = (zrecv[c, k].astype(F32) + zrecv[c, 2 + k].astype(F32)).astype(BF16)
            for q in range(CHUNKS):
                obuf[c, k, :, q * chunk : (q + 1) * chunk] = whole[q * tok : (q + 1) * tok]

    def load_wait(c):
        @pl.when(c == 0)
        def _():
            for load in loads:
                load.wait()

    def last_only(c):
        @pl.when(s == last)
        def _():
            finish(c)

    def later_section(phase):
        def run(c):
            @pl.when(s > 0)
            def _():
                phase(c)

        return run

    def first_section(phase):
        def run(c):
            @pl.when((s == 0) & (c >= 2))
            def _():
                phase(c)

        return run

    def step(t, lag, phase):
        @pl.when((t >= lag) & (t < spans + lag))
        def _():
            phase(t - lag)

    def tick(t, carry):
        step(t, 1, gather)
        step(t, -1, first_section(dispatch_inputs))
        step(t, 0, later_section(dispatch))
        step(t, 1, load_wait)
        step(t, 1, experts_own)
        step(t, 1, gather_other)
        step(t, 1, experts)
        step(t, 1, down)
        step(t, 2, combine)
        step(t, 1, give_back)
        step(t, 3, last_only)
        return carry

    for c in range(2):

        @pl.when(s == 0)
        def _():
            dispatch_inputs(c)

        placement(c + 1, 0)

    lax.fori_loop(3, spans, placement, 0)
    lax.fori_loop(0, spans + 3, tick, 0)

    def drain(c, carry):
        wait_bytes(drecv.at[c, pl.ds(0, n_shift)], dsend_sem.at[c])
        wait_bytes(drecv.at[c, pl.ds(0, n_shift)], rsend_sem.at[c])
        wait_bytes(drecv.at[c], fsend_sem.at[c])
        wait_bytes(csend.at[c], csend_sem.at[c])

        @pl.when(s < last)
        def _():
            wait_bytes(hrecv.at[c], hsend_sem.at[c])
            wait_bytes(obuf.at[c], orecv_sem.at[c])

        @pl.when(s == last)
        def _():
            wait_bytes(zrecv.at[c, pl.ds(0, 3)], zsend_sem.at[c])

        @pl.when(s > 0)
        def _():
            wait_bytes(obuf.at[c], osend_sem.at[c])

        out_ref[0, c, :, 0:half] = obuf[c, 0]
        out_ref[0, c, :, half:width] = obuf[c, 1]
        return carry

    lax.fori_loop(0, spans, drain, 0)


def shards(inputs, norm_gain, gate_weight, up_weight, down_weight, expert_ids):
    n_section = lax.axis_size("section")
    n_expert = lax.axis_size("expert")
    split = n_expert // EXPERTS
    spans, tok, width = inputs.shape
    hidden = gate_weight.shape[-1]
    cap = tok // EXPERTS * 3 // 2
    half = width // 2
    chunk = half // CHUNKS
    group = GROUP * cap
    total = n_expert * cap
    block = CHUNKS * cap

    stride = EXPERTS * cap
    e, q, r = np.meshgrid(np.arange(EXPERTS), np.arange(CHUNKS), np.arange(cap), indexing="ij")
    key = (e * cap + r + stride * q).reshape(EXPERTS, block)
    tgt_col = key.reshape(-1, 1).astype(np.int32)
    tgt_row = np.repeat(key[:, None], split, axis=1).reshape(1, -1).astype(np.int32)
    order = np.arange(GROUP * block).reshape(GROUP, CHUNKS, cap).transpose(1, 0, 2).reshape(-1)
    perm = np.eye(GROUP * block, dtype=np.float32)[order]

    vmem = pl.BlockSpec(memory_space=pltpu.VMEM)
    hbm = pl.BlockSpec(memory_space=pl.ANY)
    dma = pltpu.SemaphoreType.DMA
    blocks = (spans, n_expert, block, chunk)
    return pl.pallas_call(
        functools.partial(kernel, n_section, split, cap),
        out_shape=jax.ShapeDtypeStruct((1, spans, tok, width), BF16),
        in_specs=[vmem] * 7 + [hbm] * 3,
        out_specs=vmem,
        scratch_shapes=[
            pltpu.VMEM((width, hidden), BF16),
            pltpu.VMEM((width, hidden), BF16),
            pltpu.VMEM((2, hidden, half), BF16),
            pltpu.VMEM((2, 1, half), F32),
            pltpu.VMEM((spans, EXPERTS * block, CHUNKS * tok), BF16),
            pltpu.VMEM((spans, CHUNKS * tok, EXPERTS * split * block), BF16),
            pltpu.VMEM((spans, CHUNKS * tok, chunk), BF16),
            pltpu.VMEM((spans, EXPERTS, block, chunk), BF16),
            pltpu.VMEM(blocks, BF16),
            pltpu.VMEM(blocks, BF16),
            pltpu.VMEM((total, width), BF16),
            pltpu.VMEM((total // group, group, 1), F32),
            pltpu.VMEM((2, total, hidden), F32),
            pltpu.VMEM((total, hidden), BF16),
            pltpu.VMEM((spans, CHUNKS, total, chunk), BF16),
            pltpu.VMEM((spans, CHUNKS, total, chunk), BF16),
            pltpu.VMEM((CHUNKS, total, chunk), F32),
            pltpu.VMEM((total // group, CHUNKS, group, chunk), BF16),
            pltpu.VMEM(blocks, BF16),
            pltpu.VMEM((spans, EXPERTS, split, block, chunk), BF16),
            pltpu.VMEM((spans, CHUNKS * tok, chunk), BF16),
            pltpu.VMEM((spans, 2, CHUNKS * tok, chunk), BF16),
            pltpu.VMEM((spans, 4, CHUNKS * tok, chunk), BF16),
            pltpu.VMEM((spans, tok, half), BF16),
            pltpu.VMEM((spans, 2, tok, half), BF16),
            dma((6,)),
            dma((spans,)),
            dma((spans, total // group)),
            dma((spans,)),
            dma((spans, total // group)),
            dma((spans,)),
            dma((spans, CHUNKS)),
            dma((spans,)),
            dma((spans,)),
            dma((spans,)),
            dma((spans,)),
            dma((spans,)),
            dma((spans,)),
            dma((spans,)),
            dma((spans,)),
        ],
        compiler_params=pltpu.CompilerParams(
            collective_id=0, has_side_effects=True, vmem_limit_bytes=56 * 2**20
        ),
        name="layers",
    )(
        inputs,
        jnp.swapaxes(expert_ids, 2, 3),
        norm_gain,
        jnp.asarray(tgt_col),
        jnp.asarray(tgt_row),
        jnp.asarray(perm, BF16),
        jnp.asarray(perm.T, BF16),
        gate_weight,
        up_weight,
        down_weight,
    )


def solution(mesh):
    placed = (
        P(None, "expert", None),
        P("section", None),
        P("section", None, ("expert", "dp")),
        P("section", None, ("expert", "dp")),
        P("section", ("expert", "dp"), None),
        P("section", None, "expert", None),
    )
    return jax.shard_map(
        shards,
        mesh=mesh,
        in_specs=placed,
        out_specs=P("section", None, "expert", None),
        check_vma=False,
    )
```

```python
import functools

import jax
import jax.numpy as jnp
import numpy as np
from jax import lax
from jax.experimental import pallas as pl
from jax.experimental.pallas import tpu as pltpu
from jax.sharding import PartitionSpec as P

MESH = pl.DeviceIdType.MESH
EXPERTS = 4
CHUNKS = 4
GROUP = 4
SHIFTS = [
    *((2, 2), (1, 2), (2, 3), (1, 3)),
    *((2, 1), (3, 2), (2, 0), (0, 2)),
    *((1, 1), (3, 3), (1, 0), (0, 3)),
    *((3, 1), (0, 1), (3, 0)),
]
F32 = jnp.float32
BF16 = jnp.bfloat16


def wait_bytes(ref, sem):
    pltpu.make_async_copy(ref, ref, sem).wait()


def kernel(
    n_section,
    split,
    cap,
    x_ref,
    ids_ref,
    gain_ref,
    tgt_col_ref,
    tgt_row_ref,
    perm_ref,
    perm_t_ref,
    wg_hbm,
    wu_hbm,
    wd_hbm,
    out_ref,
    wg,
    wu,
    wd,
    gain,
    place,
    place_t,
    hbuf,
    dsend,
    drecv,
    dother,
    rows,
    squares,
    sums,
    act,
    csend,
    crecv,
    own,
    packed,
    rsend,
    rrecv,
    hsend,
    hrecv,
    zrecv,
    ostage,
    obuf,
    wsem,
    dsend_sem,
    drecv_sem,
    fsend_sem,
    frecv_sem,
    csend_sem,
    crecv_sem,
    rsend_sem,
    rrecv_sem,
    hsend_sem,
    hrecv_sem,
    zsend_sem,
    zrecv_sem,
    osend_sem,
    orecv_sem,
):
    spans, tok, width = x_ref.shape
    half = width // 2
    chunk = half // CHUNKS
    hidden = wg.shape[1]
    group = GROUP * cap
    last = n_section - 1
    s = lax.axis_index("section")
    me = lax.axis_index("expert")
    d = lax.axis_index("dp")
    core, zh = d % 2, d // 2
    ex, ey = me // split, me % split
    other = {"dp": zh * 2 + 1 - core}
    across = {"dp": (1 - zh) * 2 + core}
    opposite = {"dp": (1 - zh) * 2 + 1 - core}

    mine = pl.ds(pl.multiple_of(core * half, half), half)
    theirs = pl.ds(pl.multiple_of((1 - core) * half, half), half)
    low, high = pl.ds(0, half), pl.ds(half, half)
    loads = []
    for side, (source, target) in enumerate(((mine, low), (theirs, high))):
        loads.append((wg_hbm.at[0, source], wg.at[target]))
        loads.append((wu_hbm.at[0, source], wu.at[target]))
        loads.append((wd_hbm.at[0, :, source], wd.at[side]))
    loads = [
        pltpu.make_async_copy(source, target, wsem.at[i])
        for i, (source, target) in enumerate(loads)
    ]
    for load in loads:
        load.start()

    shifts = SHIFTS
    turned = [(-jy % split, -jx % EXPERTS) for jx, jy in shifts]

    def by_core(a, b):
        return a + core * (b - a)

    def sending(k):
        (jx, jy), (kx, ky) = shifts[k], turned[k]
        return by_core(k, shifts.index(turned[k])), by_core(jx, kx), by_core(jy, ky)

    n_shift = len(shifts)
    groups = (n_shift + 1) // GROUP

    def peer(jx, jy):
        return {"expert": ((ex + jx + EXPERTS) % EXPERTS) * split + (ey + jy + split) % split}

    barrier = pltpu.get_barrier_semaphore()

    def greet(device):
        pl.semaphore_signal(barrier, inc=1, device_id=device, device_id_type=MESH)

    def section_peers(section):
        return [
            {"section": section, "dp": zh * 2 + core},
            {"section": section, "dp": zh * 2 + 1 - core},
            {"section": section, "dp": (1 - zh) * 2 + core},
        ]

    for jx, jy in shifts:
        greet(peer(jx, jy))
    greet(other)
    greet(across)
    greet(opposite)

    @pl.when(s < last)
    def _():
        for device in section_peers(s + 1):
            greet(device)

    @pl.when(s > 0)
    def _():
        for device in section_peers(s - 1):
            greet(device)

    gain[0] = gain_ref[:, mine].astype(F32)
    gain[1] = gain_ref[:, theirs].astype(F32)

    def placement(c, carry):
        n = CHUNKS * tok
        row = lax.broadcasted_iota(jnp.int32, (n, n), 0)
        col = lax.broadcasted_iota(jnp.int32, (n, n), 1)
        token = lax.broadcasted_iota(jnp.int32, (n, tok), 0) % tok
        listed = lax.broadcasted_iota(jnp.int32, (n, tok), 1)
        ids_col = jnp.sum(jnp.where(token == listed, ids_ref[0, c], 0), axis=1, keepdims=True)
        ids_row = jnp.sum(jnp.where(row == col, ids_col, 0), axis=0, keepdims=True)
        same = (ids_col == ids_row) & (row // tok == col // tok)
        rank_row = jnp.sum((same & (row < col)).astype(jnp.int32), axis=0, keepdims=True)
        rank_col = jnp.sum((same & (col < row)).astype(jnp.int32), axis=1, keepdims=True)
        stride = EXPERTS * cap
        key_row = ids_row * cap + rank_row + stride * (col[0:1] // tok)
        key_col = ids_col * cap + rank_col + stride * (row[:, 0:1] // tok)
        place[c] = (tgt_col_ref[...] == key_row).astype(F32).astype(BF16)
        place_t[c] = (tgt_row_ref[...] == key_col).astype(F32).astype(BF16)
        return carry

    placement(0, 0)

    expected = len(shifts) + 3 + 3 * (s < last).astype(jnp.int32) + 3 * (s > 0).astype(jnp.int32)
    pl.semaphore_wait(barrier, expected)

    def remote(source, target, send_sem, recv_sem, device):
        pltpu.make_async_remote_copy(
            src_ref=source,
            dst_ref=target,
            send_sem=send_sem,
            recv_sem=recv_sem,
            device_id=device,
            device_id_type=MESH,
        ).start()

    def send_rows(c):
        sent = jnp.dot(place[c], hbuf[c], preferred_element_type=F32).astype(BF16)
        dsend[c] = sent.reshape(EXPERTS, CHUNKS * cap, chunk)
        for k in range(n_shift):
            slot, jx, jy = sending(k)
            remote(
                dsend.at[c, (ex + jx) % EXPERTS],
                drecv.at[c, slot],
                dsend_sem.at[c],
                drecv_sem.at[c, k // GROUP],
                peer(jx, jy),
            )
        pltpu.make_async_copy(
            dsend.at[c, ex], drecv.at[c, n_shift], drecv_sem.at[c, groups - 1]
        ).start()

    def dispatch_inputs(c):
        for q in range(CHUNKS):
            cols = pl.ds(pl.multiple_of(core * half + q * chunk, chunk), chunk)
            hbuf[c, q * tok : (q + 1) * tok] = x_ref[c, :, cols]
        send_rows(c)

    def dispatch(c):
        wait_bytes(hrecv.at[c], hrecv_sem.at[c])
        hbuf[c] = (hrecv[c, 0].astype(F32) + hrecv[c, 1].astype(F32)).astype(BF16)
        send_rows(c)
        for q in range(CHUNKS):
            ostage[c, :, q * chunk : (q + 1) * chunk] = hbuf[c, q * tok : (q + 1) * tok]
        for k in range(2):
            remote(
                ostage.at[c],
                obuf.at[c, core],
                osend_sem.at[c],
                orecv_sem.at[c],
                {"section": s - 1, "dp": zh * 2 + k},
            )

    def unpack(source, i, side):
        z = jnp.dot(
            perm_ref[...], source.reshape(GROUP * CHUNKS * cap, chunk), preferred_element_type=F32
        )
        total = jnp.zeros((group, 1), F32)
        for q in range(CHUNKS):
            part = z[q * group : (q + 1) * group]
            cols = slice(q * chunk, (q + 1) * chunk)
            place_at = slice(side * half + q * chunk, side * half + (q + 1) * chunk)
            rows[i * group : (i + 1) * group, place_at] = (part * gain[side, :, cols]).astype(BF16)
            total = total + jnp.sum(part * part, axis=1, keepdims=True)
        return total

    def gather(c):
        for i in range(groups):
            here = pl.ds(i * GROUP, GROUP)
            wait_bytes(drecv.at[c, here], drecv_sem.at[c, i])
            remote(drecv.at[c, here], dother.at[c, here], fsend_sem.at[c], frecv_sem.at[c, i], other)
            squares[i] = unpack(drecv[c, i * GROUP : (i + 1) * GROUP], i, 0)

    def gather_other(c):
        for i in range(groups):
            here = pl.ds(i * GROUP, GROUP)
            wait_bytes(dother.at[c, here], frecv_sem.at[c, i])
            squares[i] = squares[i] + unpack(dother[c, i * GROUP : (i + 1) * GROUP], i, 1)

    def experts_own(c):
        for cols in (slice(0, hidden),):
            sums[0, :, cols] = jnp.dot(
                rows[:, 0:half], wg[0:half, cols], preferred_element_type=F32
            )
            sums[1, :, cols] = jnp.dot(
                rows[:, 0:half], wu[0:half, cols], preferred_element_type=F32
            )

    def experts(c):
        total = squares[...].reshape(groups * group, 1)
        scale = lax.rsqrt(total / width + 1e-5)
        for cols in (slice(0, hidden),):
            gate = sums[0, :, cols] + jnp.dot(
                rows[:, half:width], wg[half:width, cols], preferred_element_type=F32
            )
            upper = sums[1, :, cols] + jnp.dot(
                rows[:, half:width], wu[half:width, cols], preferred_element_type=F32
            )
            gate = gate * scale
            gate = 0.5 * gate
            act[:, cols] = (gate * (1.0 + jnp.tanh(gate)) * (upper * scale)).astype(BF16)
        for q in range(CHUNKS):
            cols = slice(q * chunk, (q + 1) * chunk)
            csend[c, q] = jnp.dot(act[...], wd[1, :, cols], preferred_element_type=F32).astype(BF16)
            remote(csend.at[c, q], crecv.at[c, q], csend_sem.at[c], crecv_sem.at[c, q], other)

    def down(c):
        for q in range(CHUNKS):
            cols = slice(q * chunk, (q + 1) * chunk)
            own[q] = jnp.dot(act[...], wd[0, :, cols], preferred_element_type=F32)

    def give_back(c):
        for q in range(CHUNKS):
            wait_bytes(crecv.at[c, q], crecv_sem.at[c, q])
            both = (own[q] + crecv[c, q].astype(F32)).astype(BF16)
            for i in range(groups):
                packed[i, q] = both[i * group : (i + 1) * group]
        for i in range(groups):
            out = jnp.dot(
                perm_t_ref[...],
                packed[i].reshape(CHUNKS * group, chunk),
                preferred_element_type=F32,
            ).astype(BF16)
            rsend[c, i * GROUP : (i + 1) * GROUP] = out.reshape(GROUP, CHUNKS * cap, chunk)
            for k in range(i * GROUP, min(n_shift, (i + 1) * GROUP)):
                slot, jx, jy = sending(k)
                remote(
                    rsend.at[c, slot],
                    rrecv.at[c, ex, ey],
                    rsend_sem.at[c],
                    rrecv_sem.at[c],
                    peer(-jx, -jy),
                )
        pltpu.make_async_copy(rsend.at[c, n_shift], rrecv.at[c, ex, ey], rrecv_sem.at[c]).start()

    def combine(c):
        wait_bytes(rrecv.at[c], rrecv_sem.at[c])
        back = rrecv[c].reshape(EXPERTS * split * CHUNKS * cap, chunk)
        update = jnp.dot(place_t[c], back, preferred_element_type=F32)
        base = hbuf[c].astype(F32) * (zh == 0).astype(F32)
        hsend[c] = (base + update).astype(BF16)

        @pl.when(s < last)
        def _():
            for k in range(2):
                remote(
                    hsend.at[c],
                    hrecv.at[c, zh],
                    hsend_sem.at[c],
                    hrecv_sem.at[c],
                    {"section": s + 1, "dp": (1 - zh if k == 0 else zh) * 2 + core},
                )

        @pl.when(s == last)
        def _():
            zrecv[c, d] = hsend[c]
            for device in (across, opposite, other):
                remote(
                    hsend.at[c], zrecv.at[c, d], zsend_sem.at[c], zrecv_sem.at[c], device
                )

    def finish(c):
        wait_bytes(zrecv.at[c, pl.ds(0, 3)], zrecv_sem.at[c])
        for k in range(2):
            whole = (zrecv[c, k].astype(F32) + zrecv[c, 2 + k].astype(F32)).astype(BF16)
            for q in range(CHUNKS):
                obuf[c, k, :, q * chunk : (q + 1) * chunk] = whole[q * tok : (q + 1) * tok]

    def load_wait(c):
        @pl.when(c == 0)
        def _():
            for load in loads:
                load.wait()

    def last_only(c):
        @pl.when(s == last)
        def _():
            finish(c)

    def later_section(phase):
        def run(c):
            @pl.when(s > 0)
            def _():
                phase(c)

        return run

    def first_section(phase):
        def run(c):
            @pl.when((s == 0) & (c >= 2))
            def _():
                phase(c)

        return run

    def step(t, lag, phase):
        @pl.when((t >= lag) & (t < spans + lag))
        def _():
            phase(t - lag)

    def tick(t, carry):
        step(t, 1, gather)
        step(t, -1, first_section(dispatch_inputs))
        step(t, 0, later_section(dispatch))
        step(t, 1, load_wait)
        step(t, 1, experts_own)
        step(t, 1, gather_other)
        step(t, 1, experts)
        step(t, 1, down)
        step(t, 2, combine)
        step(t, 1, give_back)
        step(t, 3, last_only)
        return carry

    for c in range(2):

        @pl.when(s == 0)
        def _():
            dispatch_inputs(c)

        placement(c + 1, 0)

    lax.fori_loop(3, spans, placement, 0)
    lax.fori_loop(0, spans + 3, tick, 0)

    def drain(c, carry):
        wait_bytes(drecv.at[c, pl.ds(0, n_shift)], dsend_sem.at[c])
        wait_bytes(drecv.at[c, pl.ds(0, n_shift)], rsend_sem.at[c])
        wait_bytes(drecv.at[c], fsend_sem.at[c])
        wait_bytes(csend.at[c], csend_sem.at[c])

        @pl.when(s < last)
        def _():
            wait_bytes(hrecv.at[c], hsend_sem.at[c])
            wait_bytes(obuf.at[c], orecv_sem.at[c])

        @pl.when(s == last)
        def _():
            wait_bytes(zrecv.at[c, pl.ds(0, 3)], zsend_sem.at[c])

        @pl.when(s > 0)
        def _():
            wait_bytes(obuf.at[c], osend_sem.at[c])

        out_ref[0, c, :, 0:half] = obuf[c, 0]
        out_ref[0, c, :, half:width] = obuf[c, 1]
        return carry

    lax.fori_loop(0, spans, drain, 0)


def shards(inputs, norm_gain, gate_weight, up_weight, down_weight, expert_ids):
    n_section = lax.axis_size("section")
    n_expert = lax.axis_size("expert")
    split = n_expert // EXPERTS
    spans, tok, width = inputs.shape
    hidden = gate_weight.shape[-1]
    cap = tok // EXPERTS * 3 // 2
    half = width // 2
    chunk = half // CHUNKS
    group = GROUP * cap
    total = n_expert * cap
    block = CHUNKS * cap

    stride = EXPERTS * cap
    e, q, r = np.meshgrid(np.arange(EXPERTS), np.arange(CHUNKS), np.arange(cap), indexing="ij")
    key = (e * cap + r + stride * q).reshape(EXPERTS, block)
    tgt_col = key.reshape(-1, 1).astype(np.int32)
    tgt_row = np.repeat(key[:, None], split, axis=1).reshape(1, -1).astype(np.int32)
    order = np.arange(GROUP * block).reshape(GROUP, CHUNKS, cap).transpose(1, 0, 2).reshape(-1)
    perm = np.eye(GROUP * block, dtype=np.float32)[order]

    vmem = pl.BlockSpec(memory_space=pltpu.VMEM)
    hbm = pl.BlockSpec(memory_space=pl.ANY)
    dma = pltpu.SemaphoreType.DMA
    blocks = (spans, n_expert, block, chunk)
    return pl.pallas_call(
        functools.partial(kernel, n_section, split, cap),
        out_shape=jax.ShapeDtypeStruct((1, spans, tok, width), BF16),
        in_specs=[vmem] * 7 + [hbm] * 3,
        out_specs=vmem,
        scratch_shapes=[
            pltpu.VMEM((width, hidden), BF16),
            pltpu.VMEM((width, hidden), BF16),
            pltpu.VMEM((2, hidden, half), BF16),
            pltpu.VMEM((2, 1, half), F32),
            pltpu.VMEM((spans, EXPERTS * block, CHUNKS * tok), BF16),
            pltpu.VMEM((spans, CHUNKS * tok, EXPERTS * split * block), BF16),
            pltpu.VMEM((spans, CHUNKS * tok, chunk), BF16),
            pltpu.VMEM((spans, EXPERTS, block, chunk), BF16),
            pltpu.VMEM(blocks, BF16),
            pltpu.VMEM(blocks, BF16),
            pltpu.VMEM((total, width), BF16),
            pltpu.VMEM((total // group, group, 1), F32),
            pltpu.VMEM((2, total, hidden), F32),
            pltpu.VMEM((total, hidden), BF16),
            pltpu.VMEM((spans, CHUNKS, total, chunk), BF16),
            pltpu.VMEM((spans, CHUNKS, total, chunk), BF16),
            pltpu.VMEM((CHUNKS, total, chunk), F32),
            pltpu.VMEM((total // group, CHUNKS, group, chunk), BF16),
            pltpu.VMEM(blocks, BF16),
            pltpu.VMEM((spans, EXPERTS, split, block, chunk), BF16),
            pltpu.VMEM((spans, CHUNKS * tok, chunk), BF16),
            pltpu.VMEM((spans, 2, CHUNKS * tok, chunk), BF16),
            pltpu.VMEM((spans, 4, CHUNKS * tok, chunk), BF16),
            pltpu.VMEM((spans, tok, half), BF16),
            pltpu.VMEM((spans, 2, tok, half), BF16),
            dma((6,)),
            dma((spans,)),
            dma((spans, total // group)),
            dma((spans,)),
            dma((spans, total // group)),
            dma((spans,)),
            dma((spans, CHUNKS)),
            dma((spans,)),
            dma((spans,)),
            dma((spans,)),
            dma((spans,)),
            dma((spans,)),
            dma((spans,)),
            dma((spans,)),
            dma((spans,)),
        ],
        compiler_params=pltpu.CompilerParams(
            collective_id=0, has_side_effects=True, vmem_limit_bytes=56 * 2**20
        ),
        name="layers",
    )(
        inputs,
        jnp.swapaxes(expert_ids, 2, 3),
        norm_gain,
        jnp.asarray(tgt_col),
        jnp.asarray(tgt_row),
        jnp.asarray(perm, BF16),
        jnp.asarray(perm.T, BF16),
        gate_weight,
        up_weight,
        down_weight,
    )


def solution(mesh):
    placed = (
        P(None, "expert", None),
        P("section", None),
        P("section", None, ("expert", "dp")),
        P("section", None, ("expert", "dp")),
        P("section", ("expert", "dp"), None),
        P("section", None, "expert", None),
    )
    return jax.shard_map(
        shards,
        mesh=mesh,
        in_specs=placed,
        out_specs=P("section", None, "expert", None),
        check_vma=False,
    )
```

```python
import functools

import jax
import jax.numpy as jnp
import numpy as np
from jax import lax
from jax.experimental import pallas as pl
from jax.experimental.pallas import tpu as pltpu
from jax.sharding import PartitionSpec as P

MESH = pl.DeviceIdType.MESH
EXPERTS = 4
CHUNKS = 4
GROUP = 4
SHIFTS = [
    *((2, 2), (1, 2), (2, 3), (1, 3)),
    *((2, 1), (3, 2), (2, 0), (0, 2)),
    *((1, 1), (3, 3), (1, 0), (0, 3)),
    *((3, 1), (0, 1), (3, 0)),
]
F32 = jnp.float32
BF16 = jnp.bfloat16


def wait_bytes(ref, sem):
    pltpu.make_async_copy(ref, ref, sem).wait()


def kernel(
    n_section,
    split,
    cap,
    x_ref,
    ids_ref,
    gain_ref,
    tgt_col_ref,
    tgt_row_ref,
    perm_ref,
    perm_t_ref,
    wg_hbm,
    wu_hbm,
    wd_hbm,
    out_ref,
    wg,
    wu,
    wd,
    gain,
    place,
    place_t,
    hbuf,
    dsend,
    drecv,
    dother,
    rows,
    squares,
    sums,
    act,
    csend,
    crecv,
    own,
    packed,
    rsend,
    rrecv,
    hsend,
    hrecv,
    zrecv,
    ostage,
    obuf,
    wsem,
    dsend_sem,
    drecv_sem,
    fsend_sem,
    frecv_sem,
    csend_sem,
    crecv_sem,
    rsend_sem,
    rrecv_sem,
    hsend_sem,
    hrecv_sem,
    zsend_sem,
    zrecv_sem,
    osend_sem,
    orecv_sem,
):
    spans, tok, width = x_ref.shape
    half = width // 2
    chunk = half // CHUNKS
    hidden = wg.shape[1]
    group = GROUP * cap
    last = n_section - 1
    s = lax.axis_index("section")
    me = lax.axis_index("expert")
    d = lax.axis_index("dp")
    core, zh = d % 2, d // 2
    ex, ey = me // split, me % split
    other = {"dp": zh * 2 + 1 - core}
    across = {"dp": (1 - zh) * 2 + core}
    opposite = {"dp": (1 - zh) * 2 + 1 - core}

    mine = pl.ds(pl.multiple_of(core * half, half), half)
    theirs = pl.ds(pl.multiple_of((1 - core) * half, half), half)
    low, high = pl.ds(0, half), pl.ds(half, half)
    loads = []
    for side, (source, target) in enumerate(((mine, low), (theirs, high))):
        loads.append((wg_hbm.at[0, source], wg.at[target]))
        loads.append((wu_hbm.at[0, source], wu.at[target]))
        loads.append((wd_hbm.at[0, :, source], wd.at[side]))
    loads = [
        pltpu.make_async_copy(source, target, wsem.at[i])
        for i, (source, target) in enumerate(loads)
    ]
    for load in loads:
        load.start()

    shifts = SHIFTS
    turned = [(-jy % split, -jx % EXPERTS) for jx, jy in shifts]

    def by_core(a, b):
        return a + core * (b - a)

    def sending(k):
        (jx, jy), (kx, ky) = shifts[k], turned[k]
        return by_core(k, shifts.index(turned[k])), by_core(jx, kx), by_core(jy, ky)

    n_shift = len(shifts)
    groups = (n_shift + 1) // GROUP

    def peer(jx, jy):
        return {"expert": ((ex + jx + EXPERTS) % EXPERTS) * split + (ey + jy + split) % split}

    barrier = pltpu.get_barrier_semaphore()

    def greet(device):
        pl.semaphore_signal(barrier, inc=1, device_id=device, device_id_type=MESH)

    def section_peers(section):
        return [
            {"section": section, "dp": zh * 2 + core},
            {"section": section, "dp": zh * 2 + 1 - core},
            {"section": section, "dp": (1 - zh) * 2 + core},
        ]

    for jx, jy in shifts:
        greet(peer(jx, jy))
    greet(other)
    greet(across)
    greet(opposite)

    @pl.when(s < last)
    def _():
        for device in section_peers(s + 1):
            greet(device)

    @pl.when(s > 0)
    def _():
        for device in section_peers(s - 1):
            greet(device)

    gain[0] = gain_ref[:, mine].astype(F32)
    gain[1] = gain_ref[:, theirs].astype(F32)

    def placement(c, carry):
        n = CHUNKS * tok
        row = lax.broadcasted_iota(jnp.int32, (n, n), 0)
        col = lax.broadcasted_iota(jnp.int32, (n, n), 1)
        token = lax.broadcasted_iota(jnp.int32, (n, tok), 0) % tok
        listed = lax.broadcasted_iota(jnp.int32, (n, tok), 1)
        ids_col = jnp.sum(jnp.where(token == listed, ids_ref[0, c], 0), axis=1, keepdims=True)
        ids_row = jnp.sum(jnp.where(row == col, ids_col, 0), axis=0, keepdims=True)
        same = (ids_col == ids_row) & (row // tok == col // tok)
        rank_row = jnp.sum((same & (row < col)).astype(jnp.int32), axis=0, keepdims=True)
        rank_col = jnp.sum((same & (col < row)).astype(jnp.int32), axis=1, keepdims=True)
        stride = EXPERTS * cap
        key_row = ids_row * cap + rank_row + stride * (col[0:1] // tok)
        key_col = ids_col * cap + rank_col + stride * (row[:, 0:1] // tok)
        place[c] = (tgt_col_ref[...] == key_row).astype(F32).astype(BF16)
        place_t[c] = (tgt_row_ref[...] == key_col).astype(F32).astype(BF16)
        return carry

    placement(0, 0)

    expected = len(shifts) + 3 + 3 * (s < last).astype(jnp.int32) + 3 * (s > 0).astype(jnp.int32)
    pl.semaphore_wait(barrier, expected)

    def remote(source, target, send_sem, recv_sem, device):
        pltpu.make_async_remote_copy(
            src_ref=source,
            dst_ref=target,
            send_sem=send_sem,
            recv_sem=recv_sem,
            device_id=device,
            device_id_type=MESH,
        ).start()

    def send_rows(c):
        sent = jnp.dot(place[c], hbuf[c], preferred_element_type=F32).astype(BF16)
        dsend[c] = sent.reshape(EXPERTS, CHUNKS * cap, chunk)
        for k in range(n_shift):
            slot, jx, jy = sending(k)
            remote(
                dsend.at[c, (ex + jx) % EXPERTS],
                drecv.at[c, slot],
                dsend_sem.at[c],
                drecv_sem.at[c, k // GROUP],
                peer(jx, jy),
            )
        pltpu.make_async_copy(
            dsend.at[c, ex], drecv.at[c, n_shift], drecv_sem.at[c, groups - 1]
        ).start()

    def dispatch_inputs(c):
        for q in range(CHUNKS):
            cols = pl.ds(pl.multiple_of(core * half + q * chunk, chunk), chunk)
            hbuf[c, q * tok : (q + 1) * tok] = x_ref[c, :, cols]
        send_rows(c)

    def dispatch(c):
        wait_bytes(hrecv.at[c], hrecv_sem.at[c])
        hbuf[c] = (hrecv[c, 0].astype(F32) + hrecv[c, 1].astype(F32)).astype(BF16)
        send_rows(c)
        for q in range(CHUNKS):
            ostage[c, :, q * chunk : (q + 1) * chunk] = hbuf[c, q * tok : (q + 1) * tok]
        for k in range(2):
            remote(
                ostage.at[c],
                obuf.at[c, core],
                osend_sem.at[c],
                orecv_sem.at[c],
                {"section": s - 1, "dp": zh * 2 + k},
            )

    def unpack(source, i, side):
        z = jnp.dot(
            perm_ref[...], source.reshape(GROUP * CHUNKS * cap, chunk), preferred_element_type=F32
        )
        total = jnp.zeros((group, 1), F32)
        for q in range(CHUNKS):
            part = z[q * group : (q + 1) * group]
            cols = slice(q * chunk, (q + 1) * chunk)
            place_at = slice(side * half + q * chunk, side * half + (q + 1) * chunk)
            rows[i * group : (i + 1) * group, place_at] = (part * gain[side, :, cols]).astype(BF16)
            total = total + jnp.sum(part * part, axis=1, keepdims=True)
        return total

    def gather(c):
        for i in range(groups):
            if i == groups - 1:
                take_other(c, 0, early)
            here = pl.ds(i * GROUP, GROUP)
            wait_bytes(drecv.at[c, here], drecv_sem.at[c, i])
            remote(drecv.at[c, here], dother.at[c, here], fsend_sem.at[c], frecv_sem.at[c, i], other)
            squares[i] = unpack(drecv[c, i * GROUP : (i + 1) * GROUP], i, 0)

    def gather_other(c):
        take_other(c, early, groups)

    early = groups - 2

    def take_other(c, begin, end):
        for i in range(begin, end):
            here = pl.ds(i * GROUP, GROUP)
            wait_bytes(dother.at[c, here], frecv_sem.at[c, i])
            squares[i] = squares[i] + unpack(dother[c, i * GROUP : (i + 1) * GROUP], i, 1)

    def experts_own(c):
        for j in range(hidden // 256):
            cols = slice(j * 256, (j + 1) * 256)
            sums[0, :, cols] = jnp.dot(
                rows[:, 0:half], wg[0:half, cols], preferred_element_type=F32
            )
            sums[1, :, cols] = jnp.dot(
                rows[:, 0:half], wu[0:half, cols], preferred_element_type=F32
            )

    def experts(c):
        total = squares[...].reshape(groups * group, 1)
        scale = lax.rsqrt(total / width + 1e-5)
        for j in range(hidden // 256):
            cols = slice(j * 256, (j + 1) * 256)
            gate = sums[0, :, cols] + jnp.dot(
                rows[:, half:width], wg[half:width, cols], preferred_element_type=F32
            )
            upper = sums[1, :, cols] + jnp.dot(
                rows[:, half:width], wu[half:width, cols], preferred_element_type=F32
            )
            gate = gate * scale
            act[:, cols] = (gate / (1.0 + jnp.exp(-gate)) * (upper * scale)).astype(BF16)
        for q in range(CHUNKS):
            cols = slice(q * chunk, (q + 1) * chunk)
            csend[c, q] = jnp.dot(act[...], wd[1, :, cols], preferred_element_type=F32).astype(BF16)
            remote(csend.at[c, q], crecv.at[c, q], csend_sem.at[c], crecv_sem.at[c, q], other)

    def down(c):
        for q in range(CHUNKS):
            cols = slice(q * chunk, (q + 1) * chunk)
            own[q] = jnp.dot(act[...], wd[0, :, cols], preferred_element_type=F32)

    def give_back(c):
        for q in range(CHUNKS):
            wait_bytes(crecv.at[c, q], crecv_sem.at[c, q])
            both = (own[q] + crecv[c, q].astype(F32)).astype(BF16)
            for i in range(groups):
                packed[i, q] = both[i * group : (i + 1) * group]
        for i in range(groups):
            out = jnp.dot(
                perm_t_ref[...],
                packed[i].reshape(CHUNKS * group, chunk),
                preferred_element_type=F32,
            ).astype(BF16)
            rsend[c, i * GROUP : (i + 1) * GROUP] = out.reshape(GROUP, CHUNKS * cap, chunk)
            for k in range(i * GROUP, min(n_shift, (i + 1) * GROUP)):
                slot, jx, jy = sending(k)
                remote(
                    rsend.at[c, slot],
                    rrecv.at[c, ex, ey],
                    rsend_sem.at[c],
                    rrecv_sem.at[c],
                    peer(-jx, -jy),
                )
        pltpu.make_async_copy(rsend.at[c, n_shift], rrecv.at[c, ex, ey], rrecv_sem.at[c]).start()

    def combine(c):
        wait_bytes(rrecv.at[c], rrecv_sem.at[c])
        back = rrecv[c].reshape(EXPERTS * split * CHUNKS * cap, chunk)
        update = jnp.dot(place_t[c], back, preferred_element_type=F32)
        base = hbuf[c].astype(F32) * (zh == 0).astype(F32)
        hsend[c] = (base + update).astype(BF16)

        @pl.when(s < last)
        def _():
            for k in range(2):
                remote(
                    hsend.at[c],
                    hrecv.at[c, zh],
                    hsend_sem.at[c],
                    hrecv_sem.at[c],
                    {"section": s + 1, "dp": (1 - zh if k == 0 else zh) * 2 + core},
                )

        @pl.when(s == last)
        def _():
            zrecv[c, d] = hsend[c]
            for device in (across, opposite, other):
                remote(
                    hsend.at[c], zrecv.at[c, d], zsend_sem.at[c], zrecv_sem.at[c], device
                )

    def finish(c):
        wait_bytes(zrecv.at[c, pl.ds(0, 3)], zrecv_sem.at[c])
        for k in range(2):
            whole = (zrecv[c, k].astype(F32) + zrecv[c, 2 + k].astype(F32)).astype(BF16)
            for q in range(CHUNKS):
                obuf[c, k, :, q * chunk : (q + 1) * chunk] = whole[q * tok : (q + 1) * tok]

    def load_wait(c):
        @pl.when(c == 0)
        def _():
            for load in loads:
                load.wait()

    def last_only(c):
        @pl.when(s == last)
        def _():
            finish(c)

    def later_section(phase):
        def run(c):
            @pl.when(s > 0)
            def _():
                phase(c)

        return run

    def first_section(phase):
        def run(c):
            @pl.when((s == 0) & (c >= 2))
            def _():
                phase(c)

        return run

    def step(t, lag, phase):
        @pl.when((t >= lag) & (t < spans + lag))
        def _():
            phase(t - lag)

    def tick(t, carry):
        step(t, 1, gather)
        step(t, -1, first_section(dispatch_inputs))
        step(t, 0, later_section(dispatch))
        step(t, 1, load_wait)
        step(t, 1, experts_own)
        step(t, 1, gather_other)
        step(t, 1, experts)
        step(t, 1, down)
        step(t, 2, combine)
        step(t, 1, give_back)
        step(t, 3, last_only)
        return carry

    for c in range(2):

        @pl.when(s == 0)
        def _():
            dispatch_inputs(c)

        placement(c + 1, 0)

    lax.fori_loop(3, spans, placement, 0)
    lax.fori_loop(0, spans + 3, tick, 0)

    def drain(c, carry):
        wait_bytes(drecv.at[c, pl.ds(0, n_shift)], dsend_sem.at[c])
        wait_bytes(drecv.at[c, pl.ds(0, n_shift)], rsend_sem.at[c])
        wait_bytes(drecv.at[c], fsend_sem.at[c])
        wait_bytes(csend.at[c], csend_sem.at[c])

        @pl.when(s < last)
        def _():
            wait_bytes(hrecv.at[c], hsend_sem.at[c])
            wait_bytes(obuf.at[c], orecv_sem.at[c])

        @pl.when(s == last)
        def _():
            wait_bytes(zrecv.at[c, pl.ds(0, 3)], zsend_sem.at[c])

        @pl.when(s > 0)
        def _():
            wait_bytes(obuf.at[c], osend_sem.at[c])

        out_ref[0, c, :, 0:half] = obuf[c, 0]
        out_ref[0, c, :, half:width] = obuf[c, 1]
        return carry

    lax.fori_loop(0, spans, drain, 0)


def shards(inputs, norm_gain, gate_weight, up_weight, down_weight, expert_ids):
    n_section = lax.axis_size("section")
    n_expert = lax.axis_size("expert")
    split = n_expert // EXPERTS
    spans, tok, width = inputs.shape
    hidden = gate_weight.shape[-1]
    cap = tok // EXPERTS * 3 // 2
    half = width // 2
    chunk = half // CHUNKS
    group = GROUP * cap
    total = n_expert * cap
    block = CHUNKS * cap

    stride = EXPERTS * cap
    e, q, r = np.meshgrid(np.arange(EXPERTS), np.arange(CHUNKS), np.arange(cap), indexing="ij")
    key = (e * cap + r + stride * q).reshape(EXPERTS, block)
    tgt_col = key.reshape(-1, 1).astype(np.int32)
    tgt_row = np.repeat(key[:, None], split, axis=1).reshape(1, -1).astype(np.int32)
    order = np.arange(GROUP * block).reshape(GROUP, CHUNKS, cap).transpose(1, 0, 2).reshape(-1)
    perm = np.eye(GROUP * block, dtype=np.float32)[order]

    vmem = pl.BlockSpec(memory_space=pltpu.VMEM)
    hbm = pl.BlockSpec(memory_space=pl.ANY)
    dma = pltpu.SemaphoreType.DMA
    blocks = (spans, n_expert, block, chunk)
    return pl.pallas_call(
        functools.partial(kernel, n_section, split, cap),
        out_shape=jax.ShapeDtypeStruct((1, spans, tok, width), BF16),
        in_specs=[vmem] * 7 + [hbm] * 3,
        out_specs=vmem,
        scratch_shapes=[
            pltpu.VMEM((width, hidden), BF16),
            pltpu.VMEM((width, hidden), BF16),
            pltpu.VMEM((2, hidden, half), BF16),
            pltpu.VMEM((2, 1, half), F32),
            pltpu.VMEM((spans, EXPERTS * block, CHUNKS * tok), BF16),
            pltpu.VMEM((spans, CHUNKS * tok, EXPERTS * split * block), BF16),
            pltpu.VMEM((spans, CHUNKS * tok, chunk), BF16),
            pltpu.VMEM((spans, EXPERTS, block, chunk), BF16),
            pltpu.VMEM(blocks, BF16),
            pltpu.VMEM(blocks, BF16),
            pltpu.VMEM((total, width), BF16),
            pltpu.VMEM((total // group, group, 1), F32),
            pltpu.VMEM((2, total, hidden), F32),
            pltpu.VMEM((total, hidden), BF16),
            pltpu.VMEM((spans, CHUNKS, total, chunk), BF16),
            pltpu.VMEM((spans, CHUNKS, total, chunk), BF16),
            pltpu.VMEM((CHUNKS, total, chunk), F32),
            pltpu.VMEM((total // group, CHUNKS, group, chunk), BF16),
            pltpu.VMEM(blocks, BF16),
            pltpu.VMEM((spans, EXPERTS, split, block, chunk), BF16),
            pltpu.VMEM((spans, CHUNKS * tok, chunk), BF16),
            pltpu.VMEM((spans, 2, CHUNKS * tok, chunk), BF16),
            pltpu.VMEM((spans, 4, CHUNKS * tok, chunk), BF16),
            pltpu.VMEM((spans, tok, half), BF16),
            pltpu.VMEM((spans, 2, tok, half), BF16),
            dma((6,)),
            dma((spans,)),
            dma((spans, total // group)),
            dma((spans,)),
            dma((spans, total // group)),
            dma((spans,)),
            dma((spans, CHUNKS)),
            dma((spans,)),
            dma((spans,)),
            dma((spans,)),
            dma((spans,)),
            dma((spans,)),
            dma((spans,)),
            dma((spans,)),
            dma((spans,)),
        ],
        compiler_params=pltpu.CompilerParams(
            collective_id=0, has_side_effects=True, vmem_limit_bytes=56 * 2**20
        ),
        name="layers",
    )(
        inputs,
        jnp.swapaxes(expert_ids, 2, 3),
        norm_gain,
        jnp.asarray(tgt_col),
        jnp.asarray(tgt_row),
        jnp.asarray(perm, BF16),
        jnp.asarray(perm.T, BF16),
        gate_weight,
        up_weight,
        down_weight,
    )


def solution(mesh):
    placed = (
        P(None, "expert", None),
        P("section", None),
        P("section", None, ("expert", "dp")),
        P("section", None, ("expert", "dp")),
        P("section", ("expert", "dp"), None),
        P("section", None, "expert", None),
    )
    return jax.shard_map(
        shards,
        mesh=mesh,
        in_specs=placed,
        out_specs=P("section", None, "expert", None),
        check_vma=False,
    )
```
